512 devices in a mesh: lag: 8 (over x_hi, y), col: 64 (over z, x_lo, core).
Axes of the slice: x: 4 (x_hi: 2, x_lo: 2; x = x_hi * 2 + x_lo), y: 4, z: 16, core: 2. Of those that a mesh axis runs over, the one named last changes fastest.
Arguments:
- background: bfloat16 [8, 512, 6, 64, 128], P('lag', 'col'), may hold values from -16 to 16
- obs_ensemble: bfloat16 [8, 512, 128, 128], P('lag', 'col'), may hold values from -12 to 12
- obs_value: bfloat16 [8, 512, 128], P('lag', 'col'), may hold values from -12 to 12
- obs_weight: bfloat16 [8, 512, 128], P('lag', 'col'), may hold values from 0.099609375 to 1
- obs_count: int32 [8, 512], P('lag', 'col'), may hold values from 32 to 128, as said below
Outputs:
- analysis: bfloat16 [8, 512, 6, 64, 128], P('lag', 'col')
The draws below stay inside these ranges and needn't reach their ends.
Inputs may be any that keep to these rules, and one draw needn't show every extreme that they name: `obs_count`: each slot has at least one patch with exactly 128 live observations.
All inputs are finite; a program needn't handle non-finite values.
Results may differ from the reference program's by a relative error of at most 0.006.
Values may be sent and summed in bfloat16 or wider, within the bound.
No kernel may reach another device: no remote copies, remote signals or barrier semaphores. Data moves between devices by JAX's collectives and lax.ppermute only.
A program may use at most 64 MiB of HBM per device.

```python
import math
import jax
import jax.numpy as jnp
from jax import lax

MEMBERS = 128
LEVELS = 6
COLUMNS = 64
OBS_MAX = 128
ITERS = 12
SLOTS = 8
PATCHES = 512
REACH = 4


def draw_background(key, part):
    key = jax.random.fold_in(key, 11)
    key_center, key_noise = jax.random.split(key, 2)
    shape = (SLOTS, PATCHES, LEVELS, COLUMNS, MEMBERS)
    center = jnp.clip(jax.random.normal(key_center, (SLOTS, PATCHES, LEVELS, COLUMNS, 1), jnp.float32), -4.0, 4.0)
    noise = jnp.clip(jax.random.normal(key_noise, shape, jnp.float32), -4.0, 4.0)
    position = lax.broadcasted_iota(jnp.float32, shape, 1)
    rising = 1.0 + 2.0 * position / max(PATCHES - 1, 1)
    return jnp.clip(center + rising * noise, -16.0, 16.0).astype(jnp.bfloat16)


def draw_obs_ensemble(key, part):
    key = jax.random.fold_in(key, 7)
    key_noise, key_mode, key_load, key_scale = jax.random.split(key, 4)
    shape = (SLOTS, PATCHES, OBS_MAX, MEMBERS)
    load_shape = (SLOTS, PATCHES, OBS_MAX, 1)
    member_scale = jnp.exp(jax.random.uniform(key_scale, (MEMBERS,), jnp.float32, math.log(0.2), math.log(2.0)))
    member_noise = jnp.clip(jax.random.normal(key_noise, shape, jnp.float32), -4.0, 4.0)
    mode_vector = jnp.clip(jax.random.normal(key_mode, (MEMBERS,), jnp.float32), -4.0, 4.0)
    loading = 0.7 * jnp.clip(jax.random.normal(key_load, load_shape, jnp.float32), -4.0, 4.0)
    values = member_noise * member_scale + loading * mode_vector
    return jnp.clip(values, -12.0, 12.0).astype(jnp.bfloat16)


def draw_obs_count(key, part):
    key = jax.random.fold_in(key, 5)
    key_level, key_full = jax.random.split(key)
    counts = jax.random.randint(key_level, (SLOTS, PATCHES), OBS_MAX // 4, OBS_MAX + 1)
    chosen = jax.random.randint(key_full, (SLOTS, 1), 0, PATCHES)
    patch_index = lax.broadcasted_iota(jnp.int32, (SLOTS, PATCHES), 1)
    return jnp.where(patch_index == chosen, OBS_MAX, counts).astype(jnp.int32)


def steps_of(stream_key, shape, cuts, least, top_value):
    def one(dim, shards_of):
        steps = jax.random.uniform(jax.random.fold_in(jax.random.fold_in(stream_key, 6), dim), (shards_of,), jnp.float32, least / len(cuts), top_value / len(cuts))
        return jnp.repeat(jnp.exp(steps), shape[dim] // shards_of).reshape((-1,) + (1,) * (len(shape) - dim - 1))

    loudness = one(*cuts[0])
    for cut in cuts[1:]:
        loudness = loudness * one(*cut)
    return loudness


def scatter_about(own_key, extent, scale, limit, shards=(), kind=jnp.bfloat16):
    level = steps_of(own_key, extent, shards, -0.22, 0.18) if shards else 1.0
    values = jax.random.normal(own_key, extent, jnp.float32) * scale * level
    return jnp.minimum(jnp.maximum(values, -limit), limit).astype(kind)


def setup_inputs(seed: int = 0) -> dict:
    key_of = jax.random.split(jax.random.key(seed), 6)
    return {
        "background": draw_background(jax.random.fold_in(key_of[5], 71), 0),
        "obs_ensemble": draw_obs_ensemble(jax.random.fold_in(key_of[5], 71), 0),
        "obs_value": scatter_about(key_of[2], (SLOTS, PATCHES, OBS_MAX), 2.0, 12.0, ((0, 8), (1, 64))),
        "obs_weight": jnp.clip(jnp.exp(math.log(1.0) - 2.306499 * jax.random.uniform(key_of[3], (SLOTS, PATCHES, OBS_MAX), jnp.float32) ** steps_of(key_of[3], (SLOTS, PATCHES, OBS_MAX), ((0, 8), (1, 64)), -0.2, 0.2)), 0.099609375, 1.0).astype(jnp.bfloat16),
        "obs_count": draw_obs_count(jax.random.fold_in(key_of[5], 71), 0),
    }


relaxation = 0.9
epsilon = 1e-06

def slot_terms(obs_ensemble, obs_value, weight):
    ensemble = obs_ensemble.astype(jnp.float32)
    center = lax.optimization_barrier(jnp.mean(ensemble, axis=-1, keepdims=True))
    spread = ensemble - center
    innovation = obs_value.astype(jnp.float32) - center[..., 0]
    scaled = spread * weight.astype(jnp.float32)[..., None]
    gram_sum = jnp.einsum('spok,spol->pkl', spread, scaled, precision=lax.Precision.HIGHEST)
    vector_sum = jnp.einsum('spok,spo->pk', scaled, innovation, precision=lax.Precision.HIGHEST)
    return jnp.concatenate([gram_sum, vector_sum[:, None, :]], axis=1)

def taper_band(system):
    total = system
    for offset in range(1, REACH + 1):
        taper_weight = 1.0 - offset / (REACH + 1.0)
        total = total + taper_weight * (jnp.roll(system, offset, 0) + jnp.roll(system, -offset, 0))
    return total

def square_roots(system):
    grams = system[:, :-1, :]
    vectors = system[:, -1, :]
    members = grams.shape[-1]
    identity = jnp.eye(members, dtype=jnp.float32)
    matrix = grams + (members - 1.0) * identity
    norm_bound = lax.optimization_barrier(jnp.sum(jnp.abs(matrix), axis=(1, 2)))
    root_est = matrix / norm_bound[:, None, None]
    inverse_root = jnp.broadcast_to(identity, matrix.shape)
    for sweep in range(ITERS):
        middle = 1.5 * identity - 0.5 * jnp.einsum('pij,pjk->pik', inverse_root, root_est, precision=lax.Precision.HIGHEST)
        root_est = jnp.einsum('pij,pjk->pik', root_est, middle, precision=lax.Precision.HIGHEST)
        inverse_root = jnp.einsum('pij,pjk->pik', middle, inverse_root, precision=lax.Precision.HIGHEST)
    scale_root = jnp.sqrt((members - 1.0) / norm_bound)
    inner_prod = jnp.einsum('pij,pj->pi', inverse_root, vectors, precision=lax.Precision.HIGHEST)
    mean_weight = jnp.einsum('pij,pj->pi', inverse_root, inner_prod, precision=lax.Precision.HIGHEST) / norm_bound[:, None]
    mixing = inverse_root * scale_root[:, None, None] + mean_weight[:, :, None]
    return mixing.astype(jnp.bfloat16)

def analyse_slot(slot_state, mixing):
    states = slot_state.astype(jnp.float32)
    prior_center = lax.optimization_barrier(jnp.mean(states, axis=-1, keepdims=True))
    prior_spread = (states - prior_center).astype(jnp.bfloat16)
    increment = jnp.einsum('plck,pkj->plcj', prior_spread.astype(jnp.float32), mixing.astype(jnp.float32))
    posterior = prior_center + increment
    post_center = lax.optimization_barrier(jnp.mean(posterior, axis=-1, keepdims=True))
    post_spread = posterior - post_center
    divisor = (MEMBERS - 1.0) * PATCHES * COLUMNS
    prior_sd = jnp.sqrt(lax.optimization_barrier(jnp.sum(jnp.square(prior_spread.astype(jnp.float32)), axis=(0, 2, 3))) / divisor + epsilon)
    post_sd = jnp.sqrt(lax.optimization_barrier(jnp.sum(jnp.square(post_spread), axis=(0, 2, 3))) / divisor + epsilon)
    factor = 1.0 + relaxation * (prior_sd - post_sd) / post_sd
    return (post_center + factor[None, :, None, None] * post_spread).astype(jnp.bfloat16)

def reference(background, obs_ensemble, obs_value, obs_weight, obs_count):
    live_slots = lax.broadcasted_iota(jnp.int32, obs_value.shape, 2) < obs_count[:, :, None]
    weight = jnp.where(live_slots, obs_weight, jnp.zeros_like(obs_weight))
    system = taper_band(slot_terms(obs_ensemble, obs_value, weight))
    mixing = square_roots(system)
    return lax.map(lambda slot_state: analyse_slot(slot_state, mixing), background)
```

```python
import jax
import jax.numpy as jnp
from jax import lax
from jax.experimental import pallas as pl
from jax.experimental.pallas import tpu as pltpu
from jax.sharding import PartitionSpec as P

ITERS = 12
REACH = 4
RELAXATION = 0.9
EPSILON = 1e-06
MEMBERS = 128
HALF = MEMBERS // 2
PACKED = 72

bf16 = jnp.bfloat16
f32 = jnp.float32


def iota2(shape, dim):
    return lax.broadcasted_iota(jnp.int32, shape, dim)


def halves(value):
    high = value.astype(bf16)
    return high, (value - high.astype(f32)).astype(bf16)


def dot(left, right):
    return jnp.dot(left, right, preferred_element_type=f32)


def pack(gram, vector):
    row, lane = iota2((HALF, MEMBERS), 0), iota2((HALF, MEMBERS), 1)
    lower = pltpu.roll(gram[HALF:], HALF, 1)
    matrix = jnp.where(lane >= row, gram[:HALF], lower)
    diagonal = jnp.sum(jnp.where(lane == row, lower, 0.0), axis=0, keepdims=True)
    tail = iota2((8, MEMBERS), 0)
    rest = jnp.where(tail == 0, diagonal, jnp.where(tail == 1, vector, 0.0))
    return jnp.concatenate([matrix, rest], axis=0)


def unpack(packed):
    row, lane = iota2((HALF, MEMBERS), 0), iota2((HALF, MEMBERS), 1)
    matrix = packed[:HALF]
    diagonal = packed[HALF : HALF + 1]
    vector = packed[HALF + 1 : HALF + 2]
    flipped = jnp.transpose(jnp.concatenate([matrix, jnp.zeros_like(matrix)], axis=0))
    upper = jnp.where(lane >= row, matrix, flipped[:HALF])
    corner = jnp.where(lane == row, diagonal, jnp.where(lane < row, matrix, flipped[:HALF]))
    lower = jnp.where(lane < HALF, flipped[HALF:], pltpu.roll(corner, HALF, 1))
    return jnp.concatenate([upper, lower], axis=0), vector


def statistics_kernel(count_ref, ensemble_ref, value_ref, weight_ref, out_ref, system_ref):
    patches = ensemble_ref.shape[0]
    lane = iota2((1, MEMBERS), 1)
    for p in range(patches):
        ensemble = ensemble_ref[p]
        weight = weight_ref[p : p + 1, :].astype(f32)
        weight = jnp.where(lane < count_ref[p], weight, 0.0)
        weighted_value = weight * value_ref[p : p + 1, :].astype(f32)
        flipped = jnp.transpose(ensemble.astype(f32)) * weight
        rows = jnp.concatenate(
            [flipped, jnp.broadcast_to(weighted_value, (16, MEMBERS))], axis=0
        )
        high, low = halves(rows)
        sums = dot(
            jnp.concatenate([high, low], axis=1), jnp.concatenate([ensemble, ensemble], axis=0)
        )
        system_ref[p] = pack(sums[:MEMBERS], sums[MEMBERS : MEMBERS + 1])
    for target in range(-REACH, patches + REACH):
        total = None
        for p in range(patches):
            distance = abs(target - p)
            if distance <= REACH:
                term = (1.0 - distance / (REACH + 1.0)) * system_ref[p]
                total = term if total is None else total + term
        if 0 <= target < patches:
            out_ref[target, 0] = total
        else:
            out_ref[target % patches, 1] = total


def statistics(obs_count, obs_ensemble, obs_value, obs_weight):
    patches = obs_ensemble.shape[0]
    vmem = pl.BlockSpec(memory_space=pltpu.VMEM)
    return pl.pallas_call(
        statistics_kernel,
        out_shape=jax.ShapeDtypeStruct((patches, 2, PACKED, MEMBERS), f32),
        in_specs=[pl.BlockSpec(memory_space=pltpu.SMEM), vmem, vmem, vmem],
        out_specs=vmem,
        scratch_shapes=[pltpu.VMEM((patches, PACKED, MEMBERS), f32)],
        compiler_params=pltpu.CompilerParams(vmem_limit_bytes=16 * 1024 * 1024),
    )(obs_count, obs_ensemble, obs_value, obs_weight)


def solver_kernel(received_ref, beside_ref, out_ref):
    total = beside_ref[...]
    for s in range(received_ref.shape[0]):
        total = total + received_ref[s, 0]
    gram, vector = unpack(total)
    scale = 1.0 / MEMBERS
    mean_row = jnp.sum(gram, axis=0, keepdims=True) * scale
    mean_column = jnp.sum(gram, axis=1, keepdims=True) * scale
    mean_all = jnp.sum(mean_row, axis=1, keepdims=True) * scale
    vector = vector - mean_row
    vector = vector - jnp.sum(vector, axis=1, keepdims=True) * scale
    shape = (MEMBERS, MEMBERS)
    identity = jnp.where(iota2(shape, 0) == iota2(shape, 1), 1.0, 0.0)
    matrix = gram - mean_row - mean_column + mean_all + (MEMBERS - 1.0) * identity
    bound = jnp.sum(jnp.sum(jnp.abs(matrix), axis=0, keepdims=True), axis=1, keepdims=True)
    state = matrix / bound
    inverse_root = None
    for sweep in range(ITERS):
        middle = 1.5 * identity - 0.5 * state
        high, low = halves(middle)
        right = jnp.concatenate(
            [jnp.concatenate([high, low], axis=1), jnp.concatenate([low, high], axis=1)], axis=0
        )

        def times_middle(left):
            product = dot(jnp.concatenate(halves(left), axis=1), right)
            return product[:, :MEMBERS] + product[:, MEMBERS:]

        if sweep < ITERS - 1:
            state = times_middle(times_middle(state))
        inverse_root = middle if sweep == 0 else times_middle(inverse_root)
    inner = jnp.sum(inverse_root * vector, axis=1, keepdims=True)
    mean_weight = jnp.sum(inverse_root * inner, axis=0, keepdims=True) / bound
    mean_weight = jnp.sum(jnp.where(identity > 0.0, mean_weight, 0.0), axis=1, keepdims=True)
    mixing = inverse_root * jnp.sqrt((MEMBERS - 1.0) / bound) + mean_weight
    out_ref[...] = jnp.broadcast_to(mixing.astype(bf16)[None], out_ref.shape)


def solver(received, beside):
    vmem = pl.BlockSpec(memory_space=pltpu.VMEM)
    return pl.pallas_call(
        solver_kernel,
        out_shape=jax.ShapeDtypeStruct((received.shape[0], MEMBERS, MEMBERS), bf16),
        in_specs=[vmem, vmem],
        out_specs=vmem,
        compiler_params=pltpu.CompilerParams(vmem_limit_bytes=16 * 1024 * 1024),
    )(received, beside)


def apply_kernel(states_ref, mixing_ref, spread_ref, center_ref, sums_ref, square_ref):
    p = pl.program_id(0)
    levels, columns = states_ref.shape[1], states_ref.shape[2]
    rows = levels * columns

    @pl.when(p == 0)
    def _():
        square_ref[...] = jnp.zeros_like(square_ref)

    states = states_ref[0].reshape(rows, MEMBERS)
    average = jnp.full((MEMBERS, MEMBERS), 1.0 / MEMBERS, bf16)
    prior_center = dot(states, average)
    prior_spread = (states.astype(f32) - prior_center).astype(bf16)
    mixing = mixing_ref[0].astype(f32)
    mixing_center = jnp.sum(mixing, axis=1, keepdims=True) * (1.0 / MEMBERS)
    spread_high, spread_low = halves(mixing - mixing_center)
    center_high, center_low = halves(jnp.broadcast_to(mixing_center, mixing.shape))
    right = jnp.concatenate(
        [
            jnp.concatenate([spread_high, center_high], axis=1),
            jnp.concatenate([spread_low, center_low], axis=1),
        ],
        axis=0,
    )
    product = dot(jnp.concatenate([prior_spread, prior_spread], axis=1), right)
    post_spread = product[:, :MEMBERS]
    spread_ref[0] = post_spread.reshape(levels, columns, MEMBERS)
    center_ref[0] = (prior_center + product[:, MEMBERS:]).reshape(levels, columns, MEMBERS)
    prior_square = jnp.square(prior_spread.astype(f32)).reshape(levels, columns // 8, 8, MEMBERS)
    post_square = jnp.square(post_spread).reshape(levels, columns // 8, 8, MEMBERS)
    square_ref[0] += jnp.sum(prior_square, axis=1)
    square_ref[1] += jnp.sum(post_square, axis=1)

    @pl.when(p == pl.num_programs(0) - 1)
    def _():
        sums = jnp.sum(square_ref[...], axis=2).reshape(2 * levels, MEMBERS)
        sums = jnp.concatenate(
            [sums, jnp.zeros((MEMBERS - 2 * levels, MEMBERS), f32)], axis=0
        )
        sums = jnp.sum(jnp.transpose(sums), axis=0, keepdims=True)
        sums_ref[...] = jnp.broadcast_to(sums, sums_ref.shape)


def apply_weights(states, mixing, receivers):
    patches, levels, columns, members = states.shape
    block = pl.BlockSpec((1, levels, columns, members), lambda p: (p, 0, 0, 0))
    return pl.pallas_call(
        apply_kernel,
        grid=(patches,),
        out_shape=(
            jax.ShapeDtypeStruct(states.shape, f32),
            jax.ShapeDtypeStruct(states.shape, f32),
            jax.ShapeDtypeStruct((receivers, members), f32),
        ),
        in_specs=[block, pl.BlockSpec((1, members, members), lambda p: (p, 0, 0))],
        out_specs=(block, block, pl.BlockSpec((receivers, members), lambda p: (0, 0))),
        scratch_shapes=[pltpu.VMEM((2, levels, 8, members), f32)],
        compiler_params=pltpu.CompilerParams(vmem_limit_bytes=16 * 1024 * 1024),
    )(states, mixing)


def finish_kernel(divisor, sums_ref, spread_ref, center_ref, out_ref):
    levels = spread_ref.shape[1]
    sums = jnp.sum(sums_ref[...], axis=0, keepdims=True)
    deviation = jnp.sqrt(sums / divisor + EPSILON)
    lane = iota2(deviation.shape, 1)
    for level in range(levels):
        prior_sd = jnp.sum(jnp.where(lane == level, deviation, 0.0), axis=1, keepdims=True)
        post_sd = jnp.sum(jnp.where(lane == levels + level, deviation, 0.0), axis=1, keepdims=True)
        factor = 1.0 + RELAXATION * (prior_sd - post_sd) / post_sd
        out_ref[0, level] = (center_ref[0, level] + factor * spread_ref[0, level]).astype(bf16)


def finish(sums, spread, center, divisor):
    patches, levels, columns, members = spread.shape
    block = pl.BlockSpec((1, levels, columns, members), lambda p: (p, 0, 0, 0))

    def kernel(*refs):
        finish_kernel(divisor, *refs)

    return pl.pallas_call(
        kernel,
        grid=(patches,),
        out_shape=jax.ShapeDtypeStruct(spread.shape, bf16),
        in_specs=[pl.BlockSpec(sums.shape, lambda p: (0, 0)), block, block],
        out_specs=block,
        compiler_params=pltpu.CompilerParams(vmem_limit_bytes=16 * 1024 * 1024),
    )(sums, spread, center)


def shards(background, obs_ensemble, obs_value, obs_weight, obs_count):
    lags, tiles = lax.axis_size("lag"), lax.axis_size("col")
    patches, columns = background.shape[1], background.shape[3]
    sent = statistics(obs_count[0], obs_ensemble[0], obs_value[0], obs_weight[0])
    received = lax.all_to_all(sent, "lag", 0, 0)
    beside = jnp.sum(received[:, 1], axis=0)
    moves = [
        (i * tiles + c, i * tiles + (c + (1 if i < REACH else -1)) % tiles)
        for i in range(lags)
        for c in range(tiles)
    ]
    beside = lax.ppermute(beside, ("lag", "col"), moves)
    mixing = lax.all_to_all(solver(received, beside), "lag", 0, 0)
    spread, center, sums = apply_weights(background[0], mixing, tiles)
    sums = lax.all_to_all(sums, "col", 0, 0, tiled=True)
    divisor = (MEMBERS - 1.0) * patches * tiles * columns
    return finish(sums, spread, center, divisor)[None]


def solution(mesh):
    placed = (
        P("lag", "col", None, None, None),
        P("lag", "col", None, None),
        P("lag", "col", None),
        P("lag", "col", None),
        P("lag", "col"),
    )
    return jax.shard_map(
        shards,
        mesh=mesh,
        in_specs=placed,
        out_specs=P("lag", "col", None, None, None),
        check_vma=False,
    )
```

```python
import jax
import jax.numpy as jnp
from jax import lax
from jax.experimental import pallas as pl
from jax.experimental.pallas import tpu as pltpu
from jax.sharding import PartitionSpec as P

ITERS = 12
REACH = 4
RELAXATION = 0.9
EPSILON = 1e-06
MEMBERS = 128
HALF = MEMBERS // 2
PACKED = 72

bf16 = jnp.bfloat16
f32 = jnp.float32


def iota2(shape, dim):
    return lax.broadcasted_iota(jnp.int32, shape, dim)


def halves(value):
    high = value.astype(bf16)
    return high, (value - high.astype(f32)).astype(bf16)


def dot(left, right):
    return jnp.dot(left, right, preferred_element_type=f32)


def pack(gram, vector):
    row, lane = iota2((HALF, MEMBERS), 0), iota2((HALF, MEMBERS), 1)
    lower = pltpu.roll(gram[HALF:], HALF, 1)
    matrix = jnp.where(lane >= row, gram[:HALF], lower)
    diagonal = jnp.sum(jnp.where(lane == row, lower, 0.0), axis=0, keepdims=True)
    tail = iota2((8, MEMBERS), 0)
    rest = jnp.where(tail == 0, diagonal, jnp.where(tail == 1, vector, 0.0))
    return jnp.concatenate([matrix, rest], axis=0)


def unpack(packed):
    row, lane = iota2((HALF, MEMBERS), 0), iota2((HALF, MEMBERS), 1)
    matrix = packed[:HALF]
    diagonal = packed[HALF : HALF + 1]
    vector = packed[HALF + 1 : HALF + 2]
    flipped = jnp.transpose(jnp.concatenate([matrix, jnp.zeros_like(matrix)], axis=0))
    upper = jnp.where(lane >= row, matrix, flipped[:HALF])
    corner = jnp.where(lane == row, diagonal, jnp.where(lane < row, matrix, flipped[:HALF]))
    lower = jnp.where(lane < HALF, flipped[HALF:], pltpu.roll(corner, HALF, 1))
    return jnp.concatenate([upper, lower], axis=0), vector


def statistics_kernel(weight_ref, weighted_ref, ensemble_hbm, out_ref, ensemble_ref, system_ref, sem):
    patches = ensemble_ref.shape[0]
    copies = [
        pltpu.make_async_copy(ensemble_hbm.at[p], ensemble_ref.at[p], sem.at[p])
        for p in range(patches)
    ]
    for copy in copies:
        copy.start()
    for p in range(patches):
        copies[p].wait()
        ensemble = ensemble_ref[p]
        flipped = jnp.transpose(ensemble.astype(f32)) * weight_ref[p : p + 1, :]
        weighted_value = jnp.broadcast_to(weighted_ref[p : p + 1, :], (16, MEMBERS))
        high, low = halves(jnp.concatenate([flipped, weighted_value], axis=0))
        sums = dot(
            jnp.concatenate([high, low], axis=1), jnp.concatenate([ensemble, ensemble], axis=0)
        )
        system_ref[p] = pack(sums[:MEMBERS], sums[MEMBERS : MEMBERS + 1])
    for target in range(-REACH, patches + REACH):
        total = None
        for p in range(patches):
            distance = abs(target - p)
            if distance <= REACH:
                term = (1.0 - distance / (REACH + 1.0)) * system_ref[p]
                total = term if total is None else total + term
        if 0 <= target < patches:
            out_ref[target, 0] = total
        else:
            out_ref[target % patches, 1] = total


VMEM = pl.BlockSpec(memory_space=pltpu.VMEM)
HBM = pl.BlockSpec(memory_space=pltpu.HBM)
PARAMS = pltpu.CompilerParams(vmem_limit_bytes=16 * 1024 * 1024)


def statistics(obs_ensemble, obs_value, obs_weight, obs_count):
    patches, observations, members = obs_ensemble.shape
    weight = jnp.where(
        iota2(obs_weight.shape, 1) < obs_count[:, None], obs_weight.astype(f32), 0.0
    )
    return pl.pallas_call(
        statistics_kernel,
        out_shape=jax.ShapeDtypeStruct((patches, 2, PACKED, members), f32),
        in_specs=[VMEM, VMEM, HBM],
        out_specs=VMEM,
        scratch_shapes=[
            pltpu.VMEM(obs_ensemble.shape, bf16),
            pltpu.VMEM((patches, PACKED, members), f32),
            pltpu.SemaphoreType.DMA((patches,)),
        ],
        compiler_params=PARAMS,
    )(weight, weight * obs_value.astype(f32), obs_ensemble)


def solver_kernel(received_ref, beside_ref, out_ref):
    total = beside_ref[...]
    for s in range(received_ref.shape[0]):
        total = total + received_ref[s, 0]
    gram, vector = unpack(total)
    scale = 1.0 / MEMBERS
    mean_row = jnp.sum(gram, axis=0, keepdims=True) * scale
    mean_column = jnp.sum(gram, axis=1, keepdims=True) * scale
    mean_all = jnp.sum(mean_row, axis=1, keepdims=True) * scale
    vector = vector - mean_row
    vector = vector - jnp.sum(vector, axis=1, keepdims=True) * scale
    shape = (MEMBERS, MEMBERS)
    identity = jnp.where(iota2(shape, 0) == iota2(shape, 1), 1.0, 0.0)
    matrix = gram - mean_row - mean_column + mean_all + (MEMBERS - 1.0) * identity
    bound = jnp.sum(jnp.sum(jnp.abs(matrix), axis=0, keepdims=True), axis=1, keepdims=True)
    state = matrix / bound
    inverse_root = None
    for sweep in range(ITERS):
        middle = 1.5 * identity - 0.5 * state
        high, low = halves(middle)
        right = jnp.concatenate(
            [jnp.concatenate([high, low], axis=1), jnp.concatenate([low, high], axis=1)], axis=0
        )

        def times_middle(left):
            product = dot(jnp.concatenate(halves(left), axis=1), right)
            return product[:, :MEMBERS] + product[:, MEMBERS:]

        if sweep < ITERS - 1:
            state = times_middle(times_middle(state))
        inverse_root = middle if sweep == 0 else times_middle(inverse_root)
    inner = jnp.sum(inverse_root * vector, axis=1, keepdims=True)
    mean_weight = jnp.sum(inverse_root * inner, axis=0, keepdims=True) / bound
    mean_weight = jnp.sum(jnp.where(identity > 0.0, mean_weight, 0.0), axis=1, keepdims=True)
    mixing = inverse_root * jnp.sqrt((MEMBERS - 1.0) / bound) + mean_weight
    out_ref[...] = jnp.broadcast_to(mixing.astype(bf16)[None], out_ref.shape)


def solver(received, beside):
    return pl.pallas_call(
        solver_kernel,
        out_shape=jax.ShapeDtypeStruct((received.shape[0], MEMBERS, MEMBERS), bf16),
        in_specs=[VMEM, VMEM],
        out_specs=VMEM,
        compiler_params=PARAMS,
    )(received, beside)


def level_sums(squares, levels):
    return jnp.sum(squares.reshape(levels, -1, 8, MEMBERS), axis=1)


def prior_kernel(states_ref, spread_ref, center_ref, square_ref):
    patches, levels, columns, _ = states_ref.shape
    average = jnp.full((MEMBERS, MEMBERS), 1.0 / MEMBERS, bf16)
    total = None
    for p in range(patches):
        states = states_ref[p].reshape(levels * columns, MEMBERS)
        center = dot(states, average)
        spread = (states.astype(f32) - center).astype(bf16)
        spread_ref[p] = spread
        center_ref[p] = center
        square = level_sums(jnp.square(spread.astype(f32)), levels)
        total = square if total is None else total + square
    square_ref[...] = total


def prior(states):
    patches, levels, columns, members = states.shape
    rows = levels * columns
    return pl.pallas_call(
        prior_kernel,
        out_shape=(
            jax.ShapeDtypeStruct((patches, rows, members), bf16),
            jax.ShapeDtypeStruct((patches, rows, members), f32),
            jax.ShapeDtypeStruct((levels, 8, members), f32),
        ),
        in_specs=[VMEM],
        out_specs=(VMEM, VMEM, VMEM),
        compiler_params=PARAMS,
        cost_estimate=pl.CostEstimate(
            flops=2 * patches * rows * members * members, bytes_accessed=1 << 22, transcendentals=0
        ),
    )(states)


def apply_kernel(mixing_ref, prior_spread_ref, prior_center_ref, prior_square_ref, spread_ref, center_ref, sums_ref):
    patches = mixing_ref.shape[0]
    levels = prior_square_ref.shape[0]
    average = jnp.full((MEMBERS, MEMBERS), 1.0 / MEMBERS, bf16)
    total = None
    for p in range(patches):
        mixing = mixing_ref[p]
        mixing_center = dot(mixing, average)
        spread_high, spread_low = halves(mixing.astype(f32) - mixing_center)
        center_high, center_low = halves(mixing_center)
        right = jnp.concatenate(
            [
                jnp.concatenate([spread_high, center_high], axis=1),
                jnp.concatenate([spread_low, center_low], axis=1),
            ],
            axis=0,
        )
        prior_spread = prior_spread_ref[p]
        product = dot(jnp.concatenate([prior_spread, prior_spread], axis=1), right)
        post_spread = product[:, :MEMBERS]
        spread_ref[p] = post_spread
        center_ref[p] = prior_center_ref[p] + product[:, MEMBERS:]
        square = level_sums(jnp.square(post_spread), levels)
        total = square if total is None else total + square
    sums = jnp.concatenate(
        [jnp.sum(prior_square_ref[...], axis=1), jnp.sum(total, axis=1),
         jnp.zeros((MEMBERS - 2 * levels, MEMBERS), f32)], axis=0
    )
    sums = jnp.sum(jnp.transpose(sums), axis=0, keepdims=True)
    sums_ref[...] = jnp.broadcast_to(sums, sums_ref.shape)


def apply_weights(mixing, prior_spread, prior_center, prior_square, receivers):
    patches, rows, members = prior_spread.shape
    return pl.pallas_call(
        apply_kernel,
        out_shape=(
            jax.ShapeDtypeStruct((patches, rows, members), f32),
            jax.ShapeDtypeStruct((patches, rows, members), f32),
            jax.ShapeDtypeStruct((receivers, members), f32),
        ),
        in_specs=[VMEM] * 4,
        out_specs=(VMEM, VMEM, VMEM),
        compiler_params=PARAMS,
    )(mixing, prior_spread, prior_center, prior_square)


def finish_kernel(divisor, sums_ref, spread_ref, center_ref, out_hbm, out_ref, out_sem):
    patches, levels, columns, _ = out_ref.shape
    sums = jnp.sum(sums_ref[...], axis=0, keepdims=True)
    deviation = jnp.sqrt(sums / divisor + EPSILON)
    lane = iota2(deviation.shape, 1)
    factors = []
    for level in range(levels):
        prior_sd = jnp.sum(jnp.where(lane == level, deviation, 0.0), axis=1, keepdims=True)
        post_sd = jnp.sum(jnp.where(lane == levels + level, deviation, 0.0), axis=1, keepdims=True)
        factors.append(1.0 + RELAXATION * (prior_sd - post_sd) / post_sd)
    copies = []
    for p in range(patches):
        for level in range(levels):
            rows = pl.ds(level * columns, columns)
            result = center_ref[p, rows] + factors[level] * spread_ref[p, rows]
            out_ref[p, level] = result.astype(bf16)
        copies.append(pltpu.make_async_copy(out_ref.at[p], out_hbm.at[p], out_sem.at[p]))
        copies[-1].start()
    for copy in copies:
        copy.wait()


def finish(sums, spread, center, shape, divisor):
    def kernel(*refs):
        finish_kernel(divisor, *refs)

    return pl.pallas_call(
        kernel,
        out_shape=jax.ShapeDtypeStruct(shape, bf16),
        in_specs=[VMEM] * 3,
        out_specs=HBM,
        scratch_shapes=[pltpu.VMEM(shape, bf16), pltpu.SemaphoreType.DMA((shape[0],))],
        compiler_params=PARAMS,
    )(sums, spread, center)


def shards(background, obs_ensemble, obs_value, obs_weight, obs_count):
    lags, tiles = lax.axis_size("lag"), lax.axis_size("col")
    patches, columns = background.shape[1], background.shape[3]
    sent = statistics(obs_ensemble[0], obs_value[0], obs_weight[0], obs_count[0])
    received = lax.all_to_all(sent, "lag", 0, 0)
    beside = jnp.sum(received[:, 1], axis=0)
    moves = [
        (i * tiles + c, i * tiles + (c + (1 if i < REACH else -1)) % tiles)
        for i in range(lags)
        for c in range(tiles)
    ]
    states, beside = lax.optimization_barrier((background[0], beside))
    beside = lax.ppermute(beside, ("lag", "col"), moves)
    prior_spread, prior_center, prior_square = prior(states)
    beside, prior_square = lax.optimization_barrier((beside, prior_square))
    mixing = lax.all_to_all(solver(received, beside), "lag", 0, 0)
    spread, center, sums = apply_weights(mixing, prior_spread, prior_center, prior_square, tiles)
    sums = lax.all_to_all(sums, "col", 0, 0, tiled=True)
    divisor = (MEMBERS - 1.0) * patches * tiles * columns
    return finish(sums, spread, center, background.shape[1:], divisor)[None]


def solution(mesh):
    placed = (
        P("lag", "col", None, None, None),
        P("lag", "col", None, None),
        P("lag", "col", None),
        P("lag", "col", None),
        P("lag", "col"),
    )
    return jax.shard_map(
        shards,
        mesh=mesh,
        in_specs=placed,
        out_specs=P("lag", "col", None, None, None),
        check_vma=False,
    )
```

```python
import jax
import jax.numpy as jnp
from jax import lax
from jax.experimental import pallas as pl
from jax.experimental.pallas import tpu as pltpu
from jax.sharding import PartitionSpec as P

ITERS = 12
REACH = 4
RELAXATION = 0.9
EPSILON = 1e-06
MEMBERS = 128
HALF = MEMBERS // 2
PACKED = 72

bf16 = jnp.bfloat16
f32 = jnp.float32


def iota2(shape, dim):
    return lax.broadcasted_iota(jnp.int32, shape, dim)


def halves(value):
    high = value.astype(bf16)
    return high, (value - high.astype(f32)).astype(bf16)


def dot(left, right):
    return jnp.dot(left, right, preferred_element_type=f32)


def pack(gram, vector):
    row, lane = iota2((HALF, MEMBERS), 0), iota2((HALF, MEMBERS), 1)
    lower = pltpu.roll(gram[HALF:], HALF, 1)
    matrix = jnp.where(lane >= row, gram[:HALF], lower)
    diagonal = jnp.sum(jnp.where(lane == row, lower, 0.0), axis=0, keepdims=True)
    tail = iota2((8, MEMBERS), 0)
    rest = jnp.where(tail == 0, diagonal, jnp.where(tail == 1, vector, 0.0))
    return jnp.concatenate([matrix, rest], axis=0)


def unpack(packed):
    row, lane = iota2((HALF, MEMBERS), 0), iota2((HALF, MEMBERS), 1)
    matrix = packed[:HALF]
    diagonal = packed[HALF : HALF + 1]
    vector = packed[HALF + 1 : HALF + 2]
    flipped = jnp.transpose(jnp.concatenate([matrix, jnp.zeros_like(matrix)], axis=0))
    upper = jnp.where(lane >= row, matrix, flipped[:HALF])
    corner = jnp.where(lane == row, diagonal, jnp.where(lane < row, matrix, flipped[:HALF]))
    lower = jnp.where(lane < HALF, flipped[HALF:], pltpu.roll(corner, HALF, 1))
    return jnp.concatenate([upper, lower], axis=0), vector


def statistics_kernel(weight_ref, weighted_ref, ensemble_ref, out_ref, system_ref):
    patches = ensemble_ref.shape[0]
    for p in range(patches):
        ensemble = ensemble_ref[p]
        flipped = jnp.transpose(ensemble.astype(f32)) * weight_ref[p : p + 1, :]
        weighted_value = jnp.broadcast_to(weighted_ref[p : p + 1, :], (16, MEMBERS))
        high, low = halves(jnp.concatenate([flipped, weighted_value], axis=0))
        sums = dot(
            jnp.concatenate([high, low], axis=1), jnp.concatenate([ensemble, ensemble], axis=0)
        )
        system_ref[p] = pack(sums[:MEMBERS], sums[MEMBERS : MEMBERS + 1])
    for target in range(-REACH, patches + REACH):
        total = None
        for p in range(patches):
            distance = abs(target - p)
            if distance <= REACH:
                term = (1.0 - distance / (REACH + 1.0)) * system_ref[p]
                total = term if total is None else total + term
        if 0 <= target < patches:
            out_ref[target, 0] = total
        else:
            out_ref[target % patches, 1] = total


VMEM = pl.BlockSpec(memory_space=pltpu.VMEM)
HBM = pl.BlockSpec(memory_space=pltpu.HBM)
PARAMS = pltpu.CompilerParams(vmem_limit_bytes=16 * 1024 * 1024)


def statistics(obs_ensemble, obs_value, obs_weight, obs_count):
    patches, observations, members = obs_ensemble.shape
    weight = jnp.where(
        iota2(obs_weight.shape, 1) < obs_count[:, None], obs_weight.astype(f32), 0.0
    )
    return pl.pallas_call(
        statistics_kernel,
        out_shape=jax.ShapeDtypeStruct((patches, 2, PACKED, members), f32),
        in_specs=[VMEM] * 3,
        out_specs=VMEM,
        scratch_shapes=[
            pltpu.VMEM((patches, PACKED, members), f32),
        ],
        compiler_params=PARAMS,
    )(weight, weight * obs_value.astype(f32), obs_ensemble)


def solver_kernel(received_ref, beside_ref, out_ref):
    total = beside_ref[...]
    for s in range(received_ref.shape[0]):
        total = total + received_ref[s, 0]
    gram, vector = unpack(total)
    scale = 1.0 / MEMBERS
    mean_row = jnp.sum(gram, axis=0, keepdims=True) * scale
    mean_column = jnp.sum(gram, axis=1, keepdims=True) * scale
    mean_all = jnp.sum(mean_row, axis=1, keepdims=True) * scale
    vector = vector - mean_row
    vector = vector - jnp.sum(vector, axis=1, keepdims=True) * scale
    shape = (MEMBERS, MEMBERS)
    identity = jnp.where(iota2(shape, 0) == iota2(shape, 1), 1.0, 0.0)
    matrix = gram - mean_row - mean_column + mean_all + (MEMBERS - 1.0) * identity
    bound = jnp.sum(jnp.sum(jnp.abs(matrix), axis=0, keepdims=True), axis=1, keepdims=True)
    state = matrix / bound
    inverse_root = None
    for sweep in range(ITERS):
        middle = 1.5 * identity - 0.5 * state
        high, low = halves(middle)
        right = jnp.concatenate(
            [jnp.concatenate([high, low], axis=1), jnp.concatenate([low, high], axis=1)], axis=0
        )

        def times_middle(left):
            product = dot(jnp.concatenate(halves(left), axis=1), right)
            return product[:, :MEMBERS] + product[:, MEMBERS:]

        if sweep < ITERS - 1:
            state = times_middle(times_middle(state))
        inverse_root = middle if sweep == 0 else times_middle(inverse_root)
    inner = jnp.sum(inverse_root * vector, axis=1, keepdims=True)
    mean_weight = jnp.sum(inverse_root * inner, axis=0, keepdims=True) / bound
    mean_weight = jnp.sum(jnp.where(identity > 0.0, mean_weight, 0.0), axis=1, keepdims=True)
    mixing = inverse_root * jnp.sqrt((MEMBERS - 1.0) / bound) + mean_weight
    out_ref[...] = jnp.broadcast_to(mixing.astype(bf16)[None], out_ref.shape)


def solver(received, beside):
    return pl.pallas_call(
        solver_kernel,
        out_shape=jax.ShapeDtypeStruct((received.shape[0], MEMBERS, MEMBERS), bf16),
        in_specs=[VMEM, VMEM],
        out_specs=VMEM,
        compiler_params=PARAMS,
    )(received, beside)


def level_sums(squares, levels):
    return jnp.sum(squares.reshape(levels, -1, 8, MEMBERS), axis=1)


def prior_kernel(states_ref, spread_ref, center_ref, square_ref):
    patches, levels, columns, _ = states_ref.shape
    average = jnp.full((MEMBERS, MEMBERS), 1.0 / MEMBERS, bf16)
    total = None
    for p in range(patches):
        states = states_ref[p].reshape(levels * columns, MEMBERS)
        center = dot(states, average)
        spread = (states.astype(f32) - center).astype(bf16)
        spread_ref[p] = spread
        center_ref[p] = center
        square = level_sums(jnp.square(spread.astype(f32)), levels)
        total = square if total is None else total + square
    square_ref[...] = total


def prior(states):
    patches, levels, columns, members = states.shape
    rows = levels * columns
    return pl.pallas_call(
        prior_kernel,
        out_shape=(
            jax.ShapeDtypeStruct((patches, rows, members), bf16),
            jax.ShapeDtypeStruct((patches, rows, members), f32),
            jax.ShapeDtypeStruct((levels, 8, members), f32),
        ),
        in_specs=[VMEM],
        out_specs=(VMEM, VMEM, VMEM),
        compiler_params=PARAMS,
        cost_estimate=pl.CostEstimate(
            flops=2 * patches * rows * members * members, bytes_accessed=1 << 22, transcendentals=0
        ),
    )(states)


def apply_kernel(mixing_ref, prior_spread_ref, prior_center_ref, prior_square_ref, spread_ref, center_ref, sums_ref):
    patches = mixing_ref.shape[0]
    levels = prior_square_ref.shape[0]
    average = jnp.full((MEMBERS, MEMBERS), 1.0 / MEMBERS, bf16)
    total = None
    for p in range(patches):
        mixing = mixing_ref[p]
        mixing_center = dot(mixing, average)
        spread_high, spread_low = halves(mixing.astype(f32) - mixing_center)
        center_high, center_low = halves(mixing_center)
        right = jnp.concatenate(
            [
                jnp.concatenate([spread_high, center_high], axis=1),
                jnp.concatenate([spread_low, center_low], axis=1),
            ],
            axis=0,
        )
        prior_spread = prior_spread_ref[p]
        product = dot(jnp.concatenate([prior_spread, prior_spread], axis=1), right)
        post_spread = product[:, :MEMBERS]
        spread_ref[p] = post_spread
        center_ref[p] = prior_center_ref[p] + product[:, MEMBERS:]
        square = level_sums(jnp.square(post_spread), levels)
        total = square if total is None else total + square
    sums = jnp.concatenate(
        [jnp.sum(prior_square_ref[...], axis=1), jnp.sum(total, axis=1),
         jnp.zeros((MEMBERS - 2 * levels, MEMBERS), f32)], axis=0
    )
    sums = jnp.sum(jnp.transpose(sums), axis=0, keepdims=True)
    sums_ref[...] = jnp.broadcast_to(sums, sums_ref.shape)


def apply_weights(mixing, prior_spread, prior_center, prior_square, receivers):
    patches, rows, members = prior_spread.shape
    return pl.pallas_call(
        apply_kernel,
        out_shape=(
            jax.ShapeDtypeStruct((patches, rows, members), f32),
            jax.ShapeDtypeStruct((patches, rows, members), f32),
            jax.ShapeDtypeStruct((receivers, members), f32),
        ),
        in_specs=[VMEM] * 4,
        out_specs=(VMEM, VMEM, VMEM),
        compiler_params=PARAMS,
    )(mixing, prior_spread, prior_center, prior_square)


def finish_kernel(divisor, sums_ref, spread_ref, center_ref, out_hbm, out_ref, out_sem):
    patches, levels, columns, _ = out_ref.shape
    sums = jnp.sum(sums_ref[...], axis=0, keepdims=True)
    deviation = jnp.sqrt(sums / divisor + EPSILON)
    lane = iota2(deviation.shape, 1)
    factors = []
    for level in range(levels):
        prior_sd = jnp.sum(jnp.where(lane == level, deviation, 0.0), axis=1, keepdims=True)
        post_sd = jnp.sum(jnp.where(lane == levels + level, deviation, 0.0), axis=1, keepdims=True)
        factors.append(1.0 + RELAXATION * (prior_sd - post_sd) / post_sd)
    copies = []
    for p in range(patches):
        for level in range(levels):
            rows = pl.ds(level * columns, columns)
            result = center_ref[p, rows] + factors[level] * spread_ref[p, rows]
            out_ref[p, level] = result.astype(bf16)
        copies.append(pltpu.make_async_copy(out_ref.at[p], out_hbm.at[p], out_sem.at[p]))
        copies[-1].start()
    for copy in copies:
        copy.wait()


def finish(sums, spread, center, shape, divisor):
    def kernel(*refs):
        finish_kernel(divisor, *refs)

    return pl.pallas_call(
        kernel,
        out_shape=jax.ShapeDtypeStruct(shape, bf16),
        in_specs=[VMEM] * 3,
        out_specs=HBM,
        scratch_shapes=[pltpu.VMEM(shape, bf16), pltpu.SemaphoreType.DMA((shape[0],))],
        compiler_params=PARAMS,
    )(sums, spread, center)


def shards(background, obs_ensemble, obs_value, obs_weight, obs_count):
    lags, tiles = lax.axis_size("lag"), lax.axis_size("col")
    patches, columns = background.shape[1], background.shape[3]
    sent = statistics(obs_ensemble[0], obs_value[0], obs_weight[0], obs_count[0])
    received = lax.all_to_all(sent, "lag", 0, 0)
    beside = jnp.sum(received[:, 1], axis=0)
    moves = [
        (i * tiles + c, i * tiles + (c + (1 if i < REACH else -1)) % tiles)
        for i in range(lags)
        for c in range(tiles)
    ]
    states, beside = lax.optimization_barrier((background[0], beside))
    beside = lax.ppermute(beside, ("lag", "col"), moves)
    prior_spread, prior_center, prior_square = prior(states)
    beside, prior_square = lax.optimization_barrier((beside, prior_square))
    mixing = lax.all_to_all(solver(received, beside), "lag", 0, 0)
    spread, center, sums = apply_weights(mixing, prior_spread, prior_center, prior_square, tiles)
    sums = lax.all_to_all(sums, "col", 0, 0, tiled=True)
    divisor = (MEMBERS - 1.0) * patches * tiles * columns
    return finish(sums, spread, center, background.shape[1:], divisor)[None]


def solution(mesh):
    placed = (
        P("lag", "col", None, None, None),
        P("lag", "col", None, None),
        P("lag", "col", None),
        P("lag", "col", None),
        P("lag", "col"),
    )
    return jax.shard_map(
        shards,
        mesh=mesh,
        in_specs=placed,
        out_specs=P("lag", "col", None, None, None),
        check_vma=False,
    )
```

```python
import jax
import jax.numpy as jnp
from jax import lax
from jax.experimental import pallas as pl
from jax.experimental.pallas import tpu as pltpu
from jax.sharding import PartitionSpec as P

ITERS = 12
REACH = 4
RELAXATION = 0.9
EPSILON = 1e-06
MEMBERS = 128
HALF = MEMBERS // 2
PACKED = 72

bf16 = jnp.bfloat16
f32 = jnp.float32


def iota2(shape, dim):
    return lax.broadcasted_iota(jnp.int32, shape, dim)


def halves(value):
    high = value.astype(bf16)
    return high, (value - high.astype(f32)).astype(bf16)


def dot(left, right):
    return jnp.dot(left, right, preferred_element_type=f32)


def pack(gram, vector):
    row, lane = iota2((HALF, MEMBERS), 0), iota2((HALF, MEMBERS), 1)
    lower = pltpu.roll(gram[HALF:], HALF, 1)
    matrix = jnp.where(lane >= row, gram[:HALF], lower)
    diagonal = jnp.sum(jnp.where(lane == row, lower, 0.0), axis=0, keepdims=True)
    tail = iota2((8, MEMBERS), 0)
    rest = jnp.where(tail == 0, diagonal, jnp.where(tail == 1, vector, 0.0))
    return jnp.concatenate([matrix, rest], axis=0)


def unpack(packed):
    row, lane = iota2((HALF, MEMBERS), 0), iota2((HALF, MEMBERS), 1)
    matrix = packed[:HALF]
    diagonal = packed[HALF : HALF + 1]
    vector = packed[HALF + 1 : HALF + 2]
    flipped = jnp.transpose(jnp.concatenate([matrix, jnp.zeros_like(matrix)], axis=0))
    upper = jnp.where(lane >= row, matrix, flipped[:HALF])
    corner = jnp.where(lane == row, diagonal, jnp.where(lane < row, matrix, flipped[:HALF]))
    lower = jnp.where(lane < HALF, flipped[HALF:], pltpu.roll(corner, HALF, 1))
    return jnp.concatenate([upper, lower], axis=0), vector


def statistics_kernel(
    count_hbm, weight_hbm, value_hbm, ensemble_hbm, out_ref,
    count_ref, weight_ref, value_ref, ensemble_ref, system_ref, sem,
):
    patches = ensemble_ref.shape[0]
    arrays = [(count_hbm, count_ref), (weight_hbm, weight_ref), (value_hbm, value_ref)]
    parts = [(ensemble_hbm, ensemble_ref)]
    copies = [
        pltpu.make_async_copy(source, target, sem.at[i])
        for i, (source, target) in enumerate(parts + arrays)
    ]
    for copy in copies:
        copy.start()
    for copy in copies[1:]:
        copy.wait()
    lane = iota2((1, MEMBERS), 1)
    for p in range(patches):
        if p == 0:
            copies[0].wait()
        weight = weight_ref[p : p + 1, :].astype(f32)
        weight = jnp.where(lane < count_ref[:, p : p + 1], weight, 0.0)
        weighted_value = weight * value_ref[p : p + 1, :].astype(f32)
        ensemble = ensemble_ref[p]
        flipped = jnp.transpose(ensemble.astype(f32)) * weight
        rows = jnp.concatenate(
            [flipped, jnp.broadcast_to(weighted_value, (16, MEMBERS))], axis=0
        )
        high, low = halves(rows)
        sums = dot(
            jnp.concatenate([high, low], axis=1), jnp.concatenate([ensemble, ensemble], axis=0)
        )
        system_ref[p] = pack(sums[:MEMBERS], sums[MEMBERS : MEMBERS + 1])
    for target in range(-REACH, patches + REACH):
        total = None
        for p in range(patches):
            distance = abs(target - p)
            if distance <= REACH:
                term = (1.0 - distance / (REACH + 1.0)) * system_ref[p]
                total = term if total is None else total + term
        if 0 <= target < patches:
            out_ref[target, 0] = total
        else:
            out_ref[target % patches, 1] = total


VMEM = pl.BlockSpec(memory_space=pltpu.VMEM)
HBM = pl.BlockSpec(memory_space=pltpu.HBM)
PARAMS = pltpu.CompilerParams(vmem_limit_bytes=16 * 1024 * 1024)


def statistics(obs_count, obs_weight, obs_value, obs_ensemble):
    patches, observations, members = obs_ensemble.shape
    operands = (obs_count, obs_weight, obs_value, obs_ensemble)
    operands = [pltpu.with_memory_space_constraint(x, pltpu.HBM) for x in operands]
    return pl.pallas_call(
        statistics_kernel,
        out_shape=jax.ShapeDtypeStruct((patches, 2, PACKED, members), f32),
        in_specs=[HBM] * 4,
        out_specs=VMEM,
        scratch_shapes=[
            pltpu.VMEM(obs_count.shape, jnp.int32),
            pltpu.VMEM(obs_weight.shape, bf16),
            pltpu.VMEM(obs_value.shape, bf16),
            pltpu.VMEM(obs_ensemble.shape, bf16),
            pltpu.VMEM((patches, PACKED, members), f32),
            pltpu.SemaphoreType.DMA((4,)),
        ],
        compiler_params=PARAMS,
    )(*operands)


def solver_kernel(received_ref, beside_ref, out_ref):
    total = beside_ref[...]
    for s in range(received_ref.shape[0]):
        total = total + received_ref[s, 0]
    gram, vector = unpack(total)
    scale = 1.0 / MEMBERS
    mean_row = jnp.sum(gram, axis=0, keepdims=True) * scale
    mean_column = jnp.sum(gram, axis=1, keepdims=True) * scale
    mean_all = jnp.sum(mean_row, axis=1, keepdims=True) * scale
    vector = vector - mean_row
    vector = vector - jnp.sum(vector, axis=1, keepdims=True) * scale
    shape = (MEMBERS, MEMBERS)
    identity = jnp.where(iota2(shape, 0) == iota2(shape, 1), 1.0, 0.0)
    matrix = gram - mean_row - mean_column + mean_all + (MEMBERS - 1.0) * identity
    bound = jnp.sum(jnp.sum(jnp.abs(matrix), axis=0, keepdims=True), axis=1, keepdims=True)
    state = matrix / bound
    inverse_root = None
    for sweep in range(ITERS):
        middle = 1.5 * identity - 0.5 * state
        high, low = halves(middle)
        right = jnp.concatenate(
            [jnp.concatenate([high, low], axis=1), jnp.concatenate([low, high], axis=1)], axis=0
        )

        def times_middle(left):
            product = dot(jnp.concatenate(halves(left), axis=1), right)
            return product[:, :MEMBERS] + product[:, MEMBERS:]

        if sweep < ITERS - 1:
            state = times_middle(times_middle(state))
        inverse_root = middle if sweep == 0 else times_middle(inverse_root)
    inner = jnp.sum(inverse_root * vector, axis=1, keepdims=True)
    mean_weight = jnp.sum(inverse_root * inner, axis=0, keepdims=True) / bound
    mean_weight = jnp.sum(jnp.where(identity > 0.0, mean_weight, 0.0), axis=1, keepdims=True)
    mixing = inverse_root * jnp.sqrt((MEMBERS - 1.0) / bound) + mean_weight
    out_ref[...] = jnp.broadcast_to(mixing.astype(bf16)[None], out_ref.shape)


def solver(received, beside):
    return pl.pallas_call(
        solver_kernel,
        out_shape=jax.ShapeDtypeStruct((received.shape[0], MEMBERS, MEMBERS), bf16),
        in_specs=[VMEM, VMEM],
        out_specs=VMEM,
        compiler_params=PARAMS,
    )(received, beside)


def level_sums(squares, levels):
    return jnp.sum(squares.reshape(levels, -1, 8, MEMBERS), axis=1)


def prior_kernel(states_ref, spread_ref, center_ref, square_ref):
    patches, levels, columns, _ = states_ref.shape
    average = jnp.full((MEMBERS, MEMBERS), 1.0 / MEMBERS, bf16)
    total = None
    for p in range(patches):
        states = states_ref[p].reshape(levels * columns, MEMBERS)
        center = dot(states, average)
        spread = (states.astype(f32) - center).astype(bf16)
        spread_ref[p] = spread
        center_ref[p] = center
        square = level_sums(jnp.square(spread.astype(f32)), levels)
        total = square if total is None else total + square
    square_ref[...] = total


def prior(states):
    patches, levels, columns, members = states.shape
    rows = levels * columns
    return pl.pallas_call(
        prior_kernel,
        out_shape=(
            jax.ShapeDtypeStruct((patches, rows, members), bf16),
            jax.ShapeDtypeStruct((patches, rows, members), f32),
            jax.ShapeDtypeStruct((levels, 8, members), f32),
        ),
        in_specs=[VMEM],
        out_specs=(VMEM, VMEM, VMEM),
        compiler_params=PARAMS,
        cost_estimate=pl.CostEstimate(
            flops=2 * patches * rows * members * members, bytes_accessed=1 << 22, transcendentals=0
        ),
    )(states)


def apply_kernel(mixing_ref, prior_spread_ref, prior_center_ref, prior_square_ref, spread_ref, center_ref, sums_ref):
    patches = mixing_ref.shape[0]
    levels = prior_square_ref.shape[0]
    average = jnp.full((MEMBERS, MEMBERS), 1.0 / MEMBERS, bf16)
    total = None
    for p in range(patches):
        mixing = mixing_ref[p]
        mixing_center = dot(mixing, average)
        spread_high, spread_low = halves(mixing.astype(f32) - mixing_center)
        center_high, center_low = halves(mixing_center)
        right = jnp.concatenate(
            [
                jnp.concatenate([spread_high, center_high], axis=1),
                jnp.concatenate([spread_low, center_low], axis=1),
            ],
            axis=0,
        )
        prior_spread = prior_spread_ref[p]
        product = dot(jnp.concatenate([prior_spread, prior_spread], axis=1), right)
        post_spread = product[:, :MEMBERS]
        spread_ref[p] = post_spread
        center_ref[p] = prior_center_ref[p] + product[:, MEMBERS:]
        square = level_sums(jnp.square(post_spread), levels)
        total = square if total is None else total + square
    sums = jnp.concatenate(
        [jnp.sum(prior_square_ref[...], axis=1), jnp.sum(total, axis=1),
         jnp.zeros((MEMBERS - 2 * levels, MEMBERS), f32)], axis=0
    )
    sums = jnp.sum(jnp.transpose(sums), axis=0, keepdims=True)
    sums_ref[...] = jnp.broadcast_to(sums, sums_ref.shape)


def apply_weights(mixing, prior_spread, prior_center, prior_square, receivers):
    patches, rows, members = prior_spread.shape
    return pl.pallas_call(
        apply_kernel,
        out_shape=(
            jax.ShapeDtypeStruct((patches, rows, members), f32),
            jax.ShapeDtypeStruct((patches, rows, members), f32),
            jax.ShapeDtypeStruct((receivers, members), f32),
        ),
        in_specs=[VMEM] * 4,
        out_specs=(VMEM, VMEM, VMEM),
        compiler_params=PARAMS,
    )(mixing, prior_spread, prior_center, prior_square)


def finish_kernel(divisor, sums_ref, spread_ref, center_ref, out_hbm, out_ref, out_sem):
    patches, levels, columns, _ = out_ref.shape
    sums = jnp.sum(sums_ref[...], axis=0, keepdims=True)
    deviation = jnp.sqrt(sums / divisor + EPSILON)
    lane = iota2(deviation.shape, 1)
    factors = []
    for level in range(levels):
        prior_sd = jnp.sum(jnp.where(lane == level, deviation, 0.0), axis=1, keepdims=True)
        post_sd = jnp.sum(jnp.where(lane == levels + level, deviation, 0.0), axis=1, keepdims=True)
        factors.append(1.0 + RELAXATION * (prior_sd - post_sd) / post_sd)
    copies = []
    for p in range(patches):
        for level in range(levels):
            rows = pl.ds(level * columns, columns)
            result = center_ref[p, rows] + factors[level] * spread_ref[p, rows]
            out_ref[p, level] = result.astype(bf16)
        copies.append(pltpu.make_async_copy(out_ref.at[p], out_hbm.at[p], out_sem.at[p]))
        copies[-1].start()
    for copy in copies:
        copy.wait()


def finish(sums, spread, center, shape, divisor):
    def kernel(*refs):
        finish_kernel(divisor, *refs)

    return pl.pallas_call(
        kernel,
        out_shape=jax.ShapeDtypeStruct(shape, bf16),
        in_specs=[VMEM] * 3,
        out_specs=HBM,
        scratch_shapes=[pltpu.VMEM(shape, bf16), pltpu.SemaphoreType.DMA((shape[0],))],
        compiler_params=PARAMS,
    )(sums, spread, center)


def shards(background, obs_ensemble, obs_value, obs_weight, obs_count):
    lags, tiles = lax.axis_size("lag"), lax.axis_size("col")
    patches, columns = background.shape[1], background.shape[3]
    sent = statistics(obs_count, obs_weight[0], obs_value[0], obs_ensemble[0])
    received = lax.all_to_all(sent, "lag", 0, 0)
    beside = jnp.sum(received[:, 1], axis=0)
    moves = [
        (i * tiles + c, i * tiles + (c + (1 if i < REACH else -1)) % tiles)
        for i in range(lags)
        for c in range(tiles)
    ]
    states, beside = lax.optimization_barrier((background[0], beside))
    beside = lax.ppermute(beside, ("lag", "col"), moves)
    prior_spread, prior_center, prior_square = prior(states)
    beside, prior_square = lax.optimization_barrier((beside, prior_square))
    mixing = lax.all_to_all(solver(received, beside), "lag", 0, 0)
    spread, center, sums = apply_weights(mixing, prior_spread, prior_center, prior_square, tiles)
    sums = lax.all_to_all(sums, "col", 0, 0, tiled=True)
    divisor = (MEMBERS - 1.0) * patches * tiles * columns
    return finish(sums, spread, center, background.shape[1:], divisor)[None]


def solution(mesh):
    placed = (
        P("lag", "col", None, None, None),
        P("lag", "col", None, None),
        P("lag", "col", None),
        P("lag", "col", None),
        P("lag", "col"),
    )
    return jax.shard_map(
        shards,
        mesh=mesh,
        in_specs=placed,
        out_specs=P("lag", "col", None, None, None),
        check_vma=False,
    )
```

```python
import jax
import jax.numpy as jnp
from jax import lax
from jax.experimental import pallas as pl
from jax.experimental.pallas import tpu as pltpu
from jax.sharding import PartitionSpec as P

ITERS = 12
REACH = 4
RELAXATION = 0.9
EPSILON = 1e-06
MEMBERS = 128
HALF = MEMBERS // 2
PACKED = 72

bf16 = jnp.bfloat16
f32 = jnp.float32


def iota2(shape, dim):
    return lax.broadcasted_iota(jnp.int32, shape, dim)


def halves(value):
    high = value.astype(bf16)
    return high, (value - high.astype(f32)).astype(bf16)


def dot(left, right):
    return jnp.dot(left, right, preferred_element_type=f32)


def cross(right):
    high, low = halves(right)
    return jnp.concatenate(
        [jnp.concatenate([high, low], axis=1), jnp.concatenate([low, high], axis=1)], axis=0
    )


def product(left, crossed):
    both = dot(jnp.concatenate(halves(left), axis=1), crossed)
    return both[:, :MEMBERS] + both[:, MEMBERS:]


def pack(gram, vector):
    row, lane = iota2((HALF, MEMBERS), 0), iota2((HALF, MEMBERS), 1)
    lower = pltpu.roll(gram[HALF:], HALF, 1)
    matrix = jnp.where(lane >= row, gram[:HALF], lower)
    diagonal = jnp.sum(jnp.where(lane == row, lower, 0.0), axis=0, keepdims=True)
    tail = iota2((8, MEMBERS), 0)
    rest = jnp.where(tail == 0, diagonal, jnp.where(tail == 1, vector, 0.0))
    return jnp.concatenate([matrix, rest], axis=0)


def unpack(packed):
    row, lane = iota2((HALF, MEMBERS), 0), iota2((HALF, MEMBERS), 1)
    matrix = packed[:HALF]
    diagonal = packed[HALF : HALF + 1]
    vector = packed[HALF + 1 : HALF + 2]
    flipped = jnp.transpose(jnp.concatenate([matrix, jnp.zeros_like(matrix)], axis=0))
    upper = jnp.where(lane >= row, matrix, flipped[:HALF])
    corner = jnp.where(lane == row, diagonal, jnp.where(lane < row, matrix, flipped[:HALF]))
    lower = jnp.where(lane < HALF, flipped[HALF:], pltpu.roll(corner, HALF, 1))
    return jnp.concatenate([upper, lower], axis=0), vector


def statistics_kernel(
    count_hbm, weight_hbm, value_hbm, ensemble_hbm, out_ref,
    count_ref, weight_ref, value_ref, ensemble_ref, system_ref, sem,
):
    patches = ensemble_ref.shape[0]
    arrays = [(count_hbm, count_ref), (weight_hbm, weight_ref), (value_hbm, value_ref)]
    parts = [(ensemble_hbm, ensemble_ref)]
    copies = [
        pltpu.make_async_copy(source, target, sem.at[i])
        for i, (source, target) in enumerate(parts + arrays)
    ]
    for copy in copies:
        copy.start()
    for copy in copies[1:]:
        copy.wait()
    lane = iota2((1, MEMBERS), 1)
    copies[0].wait()
    for p in range(patches):
        weight = weight_ref[p : p + 1, :].astype(f32)
        weight = jnp.where(lane < count_ref[:, p : p + 1], weight, 0.0)
        flipped = jnp.transpose(ensemble_ref[p].astype(f32))
        center = jnp.sum(flipped, axis=0, keepdims=True) * (1.0 / MEMBERS)
        spread = flipped - center
        innovation = value_ref[p : p + 1, :].astype(f32) - center
        innovation = jnp.broadcast_to(innovation, (16, MEMBERS))
        rows = jnp.concatenate([spread, innovation], axis=0) * weight
        both = lax.dot_general(
            jnp.concatenate(halves(rows), axis=1),
            cross(spread),
            (((1,), (1,)), ((), ())),
            preferred_element_type=f32,
        )
        sums = both[:, :MEMBERS] + both[:, MEMBERS:]
        system_ref[p] = pack(sums[:MEMBERS], sums[MEMBERS : MEMBERS + 1])
    for target in range(-REACH, patches + REACH):
        total = None
        for p in range(patches):
            distance = abs(target - p)
            if distance <= REACH:
                term = (1.0 - distance / (REACH + 1.0)) * system_ref[p]
                total = term if total is None else total + term
        if 0 <= target < patches:
            out_ref[target, 0] = total
        else:
            out_ref[target % patches, 1] = total


VMEM = pl.BlockSpec(memory_space=pltpu.VMEM)
HBM = pl.BlockSpec(memory_space=pltpu.HBM)
PARAMS = pltpu.CompilerParams(vmem_limit_bytes=16 * 1024 * 1024)


def statistics(obs_count, obs_weight, obs_value, obs_ensemble):
    patches, observations, members = obs_ensemble.shape
    operands = (obs_count, obs_weight, obs_value, obs_ensemble)
    operands = [pltpu.with_memory_space_constraint(x, pltpu.HBM) for x in operands]
    return pl.pallas_call(
        statistics_kernel,
        out_shape=jax.ShapeDtypeStruct((patches, 2, PACKED, members), f32),
        in_specs=[HBM] * 4,
        out_specs=VMEM,
        scratch_shapes=[
            pltpu.VMEM(obs_count.shape, jnp.int32),
            pltpu.VMEM(obs_weight.shape, bf16),
            pltpu.VMEM(obs_value.shape, bf16),
            pltpu.VMEM(obs_ensemble.shape, bf16),
            pltpu.VMEM((patches, PACKED, members), f32),
            pltpu.SemaphoreType.DMA((4,)),
        ],
        compiler_params=PARAMS,
    )(*operands)


def solver_kernel(received_ref, beside_ref, out_ref):
    total = beside_ref[...]
    for s in range(received_ref.shape[0]):
        total = total + received_ref[s, 0]
    gram, vector = unpack(total)
    shape = (MEMBERS, MEMBERS)
    identity = jnp.where(iota2(shape, 0) == iota2(shape, 1), 1.0, 0.0)
    matrix = gram + (MEMBERS - 1.0) * identity
    bound = jnp.sum(jnp.sum(jnp.abs(matrix), axis=0, keepdims=True), axis=1, keepdims=True)
    state = matrix / bound
    inverse_root = None
    for sweep in range(ITERS):
        middle = 1.5 * identity - 0.5 * state
        crossed = cross(middle)
        if sweep < ITERS - 1:
            state = product(product(state, crossed), crossed)
        inverse_root = middle if sweep == 0 else product(inverse_root, crossed)
    inner = jnp.sum(inverse_root * vector, axis=1, keepdims=True)
    mean_weight = jnp.sum(inverse_root * inner, axis=0, keepdims=True) / bound
    mean_weight = jnp.sum(jnp.where(identity > 0.0, mean_weight, 0.0), axis=1, keepdims=True)
    mixing = inverse_root * jnp.sqrt((MEMBERS - 1.0) / bound) + mean_weight
    out_ref[...] = jnp.broadcast_to(mixing.astype(bf16)[None], out_ref.shape)


def solver(received, beside):
    return pl.pallas_call(
        solver_kernel,
        out_shape=jax.ShapeDtypeStruct((received.shape[0], MEMBERS, MEMBERS), bf16),
        in_specs=[VMEM, VMEM],
        out_specs=VMEM,
        compiler_params=PARAMS,
    )(received, beside)


def level_sums(squares, levels):
    return jnp.sum(squares.reshape(levels, -1, 8, MEMBERS), axis=1)


def prior_kernel(states_ref, spread_ref, center_ref, square_ref):
    patches, levels, columns, _ = states_ref.shape
    average = jnp.full((MEMBERS, MEMBERS), 1.0 / MEMBERS, bf16)
    total = None
    for p in range(patches):
        states = states_ref[p].reshape(levels * columns, MEMBERS)
        center = dot(states, average)
        spread = (states.astype(f32) - center).astype(bf16)
        spread_ref[p] = spread
        center_ref[p] = center
        square = level_sums(jnp.square(spread.astype(f32)), levels)
        total = square if total is None else total + square
    square_ref[...] = total


def prior(states):
    patches, levels, columns, members = states.shape
    rows = levels * columns
    return pl.pallas_call(
        prior_kernel,
        out_shape=(
            jax.ShapeDtypeStruct((patches, rows, members), bf16),
            jax.ShapeDtypeStruct((patches, rows, members), f32),
            jax.ShapeDtypeStruct((levels, 8, members), f32),
        ),
        in_specs=[VMEM],
        out_specs=(VMEM, VMEM, VMEM),
        compiler_params=PARAMS,
        cost_estimate=pl.CostEstimate(
            flops=2 * patches * rows * members * members, bytes_accessed=1 << 22, transcendentals=0
        ),
    )(states)


def apply_kernel(mixing_ref, prior_spread_ref, prior_center_ref, prior_square_ref, spread_ref, center_ref, sums_ref):
    patches = mixing_ref.shape[0]
    levels = prior_square_ref.shape[0]
    average = jnp.full((MEMBERS, MEMBERS), 1.0 / MEMBERS, bf16)
    total = None
    for p in range(patches):
        mixing = mixing_ref[p]
        mixing_center = dot(mixing, average)
        spread_high, spread_low = halves(mixing.astype(f32) - mixing_center)
        center_high, center_low = halves(mixing_center)
        right = jnp.concatenate(
            [
                jnp.concatenate([spread_high, center_high], axis=1),
                jnp.concatenate([spread_low, center_low], axis=1),
            ],
            axis=0,
        )
        prior_spread = prior_spread_ref[p]
        both = dot(jnp.concatenate([prior_spread, prior_spread], axis=1), right)
        post_spread = both[:, :MEMBERS]
        spread_ref[p] = post_spread
        center_ref[p] = prior_center_ref[p] + both[:, MEMBERS:]
        square = level_sums(jnp.square(post_spread), levels)
        total = square if total is None else total + square
    sums = jnp.concatenate(
        [jnp.sum(prior_square_ref[...], axis=1), jnp.sum(total, axis=1),
         jnp.zeros((MEMBERS - 2 * levels, MEMBERS), f32)], axis=0
    )
    sums = jnp.sum(jnp.transpose(sums), axis=0, keepdims=True)
    sums_ref[...] = jnp.broadcast_to(sums, sums_ref.shape)


def apply_weights(mixing, prior_spread, prior_center, prior_square, receivers):
    patches, rows, members = prior_spread.shape
    return pl.pallas_call(
        apply_kernel,
        out_shape=(
            jax.ShapeDtypeStruct((patches, rows, members), f32),
            jax.ShapeDtypeStruct((patches, rows, members), f32),
            jax.ShapeDtypeStruct((receivers, members), f32),
        ),
        in_specs=[VMEM] * 4,
        out_specs=(VMEM, VMEM, VMEM),
        compiler_params=PARAMS,
    )(mixing, prior_spread, prior_center, prior_square)


def finish_kernel(divisor, sums_ref, spread_ref, center_ref, out_hbm, out_ref, out_sem):
    patches, levels, columns, _ = out_ref.shape
    sums = jnp.sum(sums_ref[...], axis=0, keepdims=True)
    deviation = jnp.sqrt(sums / divisor + EPSILON)
    lane = iota2(deviation.shape, 1)
    factors = []
    for level in range(levels):
        prior_sd = jnp.sum(jnp.where(lane == level, deviation, 0.0), axis=1, keepdims=True)
        post_sd = jnp.sum(jnp.where(lane == levels + level, deviation, 0.0), axis=1, keepdims=True)
        factors.append(1.0 + RELAXATION * (prior_sd - post_sd) / post_sd)
    copies = []
    for p in range(patches):
        for level in range(levels):
            rows = pl.ds(level * columns, columns)
            result = center_ref[p, rows] + factors[level] * spread_ref[p, rows]
            out_ref[p, level] = result.astype(bf16)
        copies.append(pltpu.make_async_copy(out_ref.at[p], out_hbm.at[p], out_sem.at[p]))
        copies[-1].start()
    for copy in copies:
        copy.wait()


def finish(sums, spread, center, shape, divisor):
    def kernel(*refs):
        finish_kernel(divisor, *refs)

    return pl.pallas_call(
        kernel,
        out_shape=jax.ShapeDtypeStruct(shape, bf16),
        in_specs=[VMEM] * 3,
        out_specs=HBM,
        scratch_shapes=[pltpu.VMEM(shape, bf16), pltpu.SemaphoreType.DMA((shape[0],))],
        compiler_params=PARAMS,
    )(sums, spread, center)


def shards(background, obs_ensemble, obs_value, obs_weight, obs_count):
    lags, tiles = lax.axis_size("lag"), lax.axis_size("col")
    patches, columns = background.shape[1], background.shape[3]
    sent = statistics(obs_count, obs_weight[0], obs_value[0], obs_ensemble[0])
    received = lax.all_to_all(sent, "lag", 0, 0)
    beside = jnp.sum(received[:, 1], axis=0)
    moves = [
        (i * tiles + c, i * tiles + (c + (1 if i < REACH else -1)) % tiles)
        for i in range(lags)
        for c in range(tiles)
    ]
    states, beside = lax.optimization_barrier((background[0], beside))
    beside = lax.ppermute(beside, ("lag", "col"), moves)
    prior_spread, prior_center, prior_square = prior(states)
    beside, prior_square = lax.optimization_barrier((beside, prior_square))
    mixing = lax.all_to_all(solver(received, beside), "lag", 0, 0)
    spread, center, sums = apply_weights(mixing, prior_spread, prior_center, prior_square, tiles)
    sums = lax.all_to_all(sums, "col", 0, 0, tiled=True)
    divisor = (MEMBERS - 1.0) * patches * tiles * columns
    return finish(sums, spread, center, background.shape[1:], divisor)[None]


def solution(mesh):
    placed = (
        P("lag", "col", None, None, None),
        P("lag", "col", None, None),
        P("lag", "col", None),
        P("lag", "col", None),
        P("lag", "col"),
    )
    return jax.shard_map(
        shards,
        mesh=mesh,
        in_specs=placed,
        out_specs=P("lag", "col", None, None, None),
        check_vma=False,
    )
```

```python
import jax
import jax.numpy as jnp
from jax import lax
from jax.experimental import pallas as pl
from jax.experimental.pallas import tpu as pltpu
from jax.sharding import PartitionSpec as P

ITERS = 12
REACH = 4
RELAXATION = 0.9
EPSILON = 1e-06
MEMBERS = 128
HALF = MEMBERS // 2
PACKED = 72
PAIR = PACKED + HALF

bf16 = jnp.bfloat16
f32 = jnp.float32


def iota2(shape, dim):
    return lax.broadcasted_iota(jnp.int32, shape, dim)


def halves(value):
    high = value.astype(bf16)
    return high, (value - high.astype(f32)).astype(bf16)


def dot(left, right):
    return jnp.dot(left, right, preferred_element_type=f32)


def crossed_halves(high, low):
    return jnp.concatenate(
        [jnp.concatenate([high, low], axis=1), jnp.concatenate([low, high], axis=1)], axis=0
    )


def cross(right):
    return crossed_halves(*halves(right))


def product(left, crossed):
    both = dot(jnp.concatenate(halves(left), axis=1), crossed)
    return both[:, :MEMBERS] + both[:, MEMBERS:]


def pack(gram, vector):
    row, lane = iota2((HALF, MEMBERS), 0), iota2((HALF, MEMBERS), 1)
    lower = pltpu.roll(gram[HALF:], HALF, 1)
    matrix = jnp.where(lane >= row, gram[:HALF], lower)
    diagonal = jnp.sum(jnp.where(lane == row, lower, 0.0), axis=0, keepdims=True)
    tail = iota2((8, MEMBERS), 0)
    rest = jnp.where(tail == 0, diagonal, jnp.where(tail == 1, vector, 0.0))
    return jnp.concatenate([matrix, rest], axis=0)


def unpack(matrix, rest):
    row, lane = iota2((HALF, MEMBERS), 0), iota2((HALF, MEMBERS), 1)
    diagonal, vector = rest[0:1], rest[1:2]
    flipped = jnp.transpose(jnp.concatenate([matrix, jnp.zeros_like(matrix)], axis=0))
    upper = jnp.where(lane >= row, matrix, flipped[:HALF])
    corner = jnp.where(lane == row, diagonal, jnp.where(lane < row, matrix, flipped[:HALF]))
    lower = jnp.where(lane < HALF, flipped[HALF:], pltpu.roll(corner, HALF, 1))
    return jnp.concatenate([upper, lower], axis=0), vector


def statistics_kernel(
    count_hbm, weight_hbm, value_hbm, ensemble_hbm, out_ref,
    count_ref, weight_ref, value_ref, ensemble_ref, system_ref, sem,
):
    patches = ensemble_ref.shape[0]
    arrays = [(count_hbm, count_ref), (weight_hbm, weight_ref), (value_hbm, value_ref)]
    parts = [(ensemble_hbm, ensemble_ref)]
    copies = [
        pltpu.make_async_copy(source, target, sem.at[i])
        for i, (source, target) in enumerate(parts + arrays)
    ]
    for copy in copies:
        copy.start()
    for copy in copies[1:]:
        copy.wait()
    lane = iota2((1, MEMBERS), 1)
    copies[0].wait()
    for p in range(patches):
        weight = weight_ref[p : p + 1, :].astype(f32)
        weight = jnp.sqrt(jnp.where(lane < count_ref[:, p : p + 1], weight, 0.0))
        flipped = jnp.transpose(ensemble_ref[p].astype(f32))
        center = jnp.sum(flipped, axis=0, keepdims=True) * (1.0 / MEMBERS)
        spread = flipped - center
        innovation = value_ref[p : p + 1, :].astype(f32) - center
        innovation = jnp.broadcast_to(innovation, (16, MEMBERS))
        high, low = halves(jnp.concatenate([spread, innovation], axis=0) * weight)
        both = lax.dot_general(
            jnp.concatenate([high, low], axis=1),
            crossed_halves(high[:MEMBERS], low[:MEMBERS]),
            (((1,), (1,)), ((), ())),
            preferred_element_type=f32,
        )
        sums = both[:, :MEMBERS] + both[:, MEMBERS:]
        system_ref[p] = pack(sums[:MEMBERS], sums[MEMBERS : MEMBERS + 1])

    def tapered(target):
        total = None
        for p in range(patches):
            distance = abs(target - p)
            if distance <= REACH:
                term = (1.0 - distance / (REACH + 1.0)) * system_ref[p]
                total = term if total is None else total + term
        return total

    for lag in range(patches):
        own = tapered(lag)
        beside = tapered(lag + patches if lag < REACH else lag - patches)
        out_ref[lag, :HALF] = own[:HALF]
        out_ref[lag, HALF:MEMBERS] = beside[:HALF]
        out_ref[lag, MEMBERS:] = own[HALF:] + pltpu.roll(beside[HALF:], 2, 0)


VMEM = pl.BlockSpec(memory_space=pltpu.VMEM)
HBM = pl.BlockSpec(memory_space=pltpu.HBM)
PARAMS = pltpu.CompilerParams(vmem_limit_bytes=16 * 1024 * 1024)


def statistics(obs_count, obs_weight, obs_value, obs_ensemble):
    patches, observations, members = obs_ensemble.shape
    operands = (obs_count, obs_weight, obs_value, obs_ensemble)
    operands = [pltpu.with_memory_space_constraint(x, pltpu.HBM) for x in operands]
    return pl.pallas_call(
        statistics_kernel,
        out_shape=jax.ShapeDtypeStruct((patches, PAIR, members), f32),
        in_specs=[HBM] * 4,
        out_specs=VMEM,
        scratch_shapes=[
            pltpu.VMEM(obs_count.shape, jnp.int32),
            pltpu.VMEM(obs_weight.shape, bf16),
            pltpu.VMEM(obs_value.shape, bf16),
            pltpu.VMEM(obs_ensemble.shape, bf16),
            pltpu.VMEM((patches, PACKED, members), f32),
            pltpu.SemaphoreType.DMA((4,)),
        ],
        compiler_params=PARAMS,
    )(*operands)


def solver_kernel(received_ref, beside_ref, out_ref):
    matrix = beside_ref[:HALF]
    rest = pltpu.roll(beside_ref[HALF:], 6, 0)
    for s in range(received_ref.shape[0]):
        matrix = matrix + received_ref[s, :HALF]
        rest = rest + received_ref[s, MEMBERS:]
    gram, vector = unpack(matrix, rest)
    shape = (MEMBERS, MEMBERS)
    identity = jnp.where(iota2(shape, 0) == iota2(shape, 1), 1.0, 0.0)
    matrix = gram + (MEMBERS - 1.0) * identity
    bound = jnp.sum(jnp.sum(jnp.abs(matrix), axis=0, keepdims=True), axis=1, keepdims=True)
    state = matrix / bound
    inverse_root = None
    for sweep in range(ITERS):
        middle = 1.5 * identity - 0.5 * state
        crossed = cross(middle)
        if sweep < ITERS - 1:
            state = product(product(state, crossed), crossed)
        inverse_root = middle if sweep == 0 else product(inverse_root, crossed)
    inner = jnp.sum(inverse_root * vector, axis=1, keepdims=True)
    mean_weight = jnp.sum(inverse_root * inner, axis=0, keepdims=True) / bound
    mean_weight = jnp.sum(jnp.where(identity > 0.0, mean_weight, 0.0), axis=1, keepdims=True)
    mixing = inverse_root * jnp.sqrt((MEMBERS - 1.0) / bound) + mean_weight
    out_ref[...] = jnp.broadcast_to(mixing.astype(bf16)[None], out_ref.shape)


def solver(received, beside):
    return pl.pallas_call(
        solver_kernel,
        out_shape=jax.ShapeDtypeStruct((received.shape[0], MEMBERS, MEMBERS), bf16),
        in_specs=[VMEM, VMEM],
        out_specs=VMEM,
        compiler_params=PARAMS,
    )(received, beside)


def level_sums(squares, levels):
    return jnp.sum(squares.reshape(levels, -1, 8, MEMBERS), axis=1)


def prior_kernel(states_ref, spread_ref, center_ref, square_ref):
    patches, levels, columns, _ = states_ref.shape
    average = jnp.full((MEMBERS, MEMBERS), 1.0 / MEMBERS, bf16)
    total = None
    for p in range(patches):
        states = states_ref[p].reshape(levels * columns, MEMBERS)
        center = dot(states, average)
        spread = (states.astype(f32) - center).astype(bf16)
        spread_ref[p] = spread
        center_ref[p] = center
        square = level_sums(jnp.square(spread.astype(f32)), levels)
        total = square if total is None else total + square
    square_ref[...] = total


def prior(states):
    patches, levels, columns, members = states.shape
    rows = levels * columns
    return pl.pallas_call(
        prior_kernel,
        out_shape=(
            jax.ShapeDtypeStruct((patches, rows, members), bf16),
            jax.ShapeDtypeStruct((patches, rows, members), f32),
            jax.ShapeDtypeStruct((levels, 8, members), f32),
        ),
        in_specs=[VMEM],
        out_specs=(VMEM, VMEM, VMEM),
        compiler_params=PARAMS,
        cost_estimate=pl.CostEstimate(
            flops=2 * patches * rows * members * members, bytes_accessed=1 << 22, transcendentals=0
        ),
    )(states)


def apply_kernel(mixing_ref, prior_spread_ref, prior_center_ref, prior_square_ref, spread_ref, center_ref, sums_ref):
    patches = mixing_ref.shape[0]
    levels = prior_square_ref.shape[0]
    average = jnp.full((MEMBERS, MEMBERS), 1.0 / MEMBERS, bf16)
    total = None
    for p in range(patches):
        mixing = mixing_ref[p]
        mixing_center = dot(mixing, average)
        spread_high, spread_low = halves(mixing.astype(f32) - mixing_center)
        center_high, center_low = halves(mixing_center)
        right = jnp.concatenate(
            [
                jnp.concatenate([spread_high, center_high], axis=1),
                jnp.concatenate([spread_low, center_low], axis=1),
            ],
            axis=0,
        )
        prior_spread = prior_spread_ref[p]
        both = dot(jnp.concatenate([prior_spread, prior_spread], axis=1), right)
        post_spread = both[:, :MEMBERS]
        spread_ref[p] = post_spread
        center_ref[p] = prior_center_ref[p] + both[:, MEMBERS:]
        square = level_sums(jnp.square(post_spread), levels)
        total = square if total is None else total + square
    sums = jnp.concatenate(
        [jnp.sum(prior_square_ref[...], axis=1), jnp.sum(total, axis=1),
         jnp.zeros((MEMBERS - 2 * levels, MEMBERS), f32)], axis=0
    )
    sums = jnp.sum(jnp.transpose(sums), axis=0, keepdims=True)
    sums_ref[...] = jnp.broadcast_to(sums, sums_ref.shape)


def apply_weights(mixing, prior_spread, prior_center, prior_square, receivers):
    patches, rows, members = prior_spread.shape
    return pl.pallas_call(
        apply_kernel,
        out_shape=(
            jax.ShapeDtypeStruct((patches, rows, members), f32),
            jax.ShapeDtypeStruct((patches, rows, members), f32),
            jax.ShapeDtypeStruct((receivers, members), f32),
        ),
        in_specs=[VMEM] * 4,
        out_specs=(VMEM, VMEM, VMEM),
        compiler_params=PARAMS,
    )(mixing, prior_spread, prior_center, prior_square)


def finish_kernel(divisor, sums_ref, spread_ref, center_ref, out_hbm, out_ref, out_sem):
    patches, levels, columns, _ = out_ref.shape
    sums = jnp.sum(sums_ref[...], axis=0, keepdims=True)
    deviation = jnp.sqrt(sums / divisor + EPSILON)
    lane = iota2(deviation.shape, 1)
    factors = []
    for level in range(levels):
        prior_sd = jnp.sum(jnp.where(lane == level, deviation, 0.0), axis=1, keepdims=True)
        post_sd = jnp.sum(jnp.where(lane == levels + level, deviation, 0.0), axis=1, keepdims=True)
        factors.append(1.0 + RELAXATION * (prior_sd - post_sd) / post_sd)
    copies = []
    for p in range(patches):
        for level in range(levels):
            rows = pl.ds(level * columns, columns)
            result = center_ref[p, rows] + factors[level] * spread_ref[p, rows]
            out_ref[p, level] = result.astype(bf16)
        copies.append(pltpu.make_async_copy(out_ref.at[p], out_hbm.at[p], out_sem.at[p]))
        copies[-1].start()
    for copy in copies:
        copy.wait()


def finish(sums, spread, center, shape, divisor):
    def kernel(*refs):
        finish_kernel(divisor, *refs)

    return pl.pallas_call(
        kernel,
        out_shape=jax.ShapeDtypeStruct(shape, bf16),
        in_specs=[VMEM] * 3,
        out_specs=HBM,
        scratch_shapes=[pltpu.VMEM(shape, bf16), pltpu.SemaphoreType.DMA((shape[0],))],
        compiler_params=PARAMS,
    )(sums, spread, center)


def shards(background, obs_ensemble, obs_value, obs_weight, obs_count):
    lags, tiles = lax.axis_size("lag"), lax.axis_size("col")
    patches, columns = background.shape[1], background.shape[3]
    sent = statistics(obs_count, obs_weight[0], obs_value[0], obs_ensemble[0])
    received = lax.all_to_all(sent, "lag", 0, 0)
    beside = jnp.sum(received[:, HALF:], axis=0)
    moves = [
        (i * tiles + c, i * tiles + (c + (1 if i < REACH else -1)) % tiles)
        for i in range(lags)
        for c in range(tiles)
    ]
    states, beside = lax.optimization_barrier((background[0], beside))
    beside = lax.ppermute(beside, ("lag", "col"), moves)
    prior_spread, prior_center, prior_square = prior(states)
    beside, prior_square = lax.optimization_barrier((beside, prior_square))
    mixing = lax.all_to_all(solver(received, beside), "lag", 0, 0)
    spread, center, sums = apply_weights(mixing, prior_spread, prior_center, prior_square, tiles)
    sums = lax.all_to_all(sums, "col", 0, 0, tiled=True)
    divisor = (MEMBERS - 1.0) * patches * tiles * columns
    return finish(sums, spread, center, background.shape[1:], divisor)[None]


def solution(mesh):
    placed = (
        P("lag", "col", None, None, None),
        P("lag", "col", None, None),
        P("lag", "col", None),
        P("lag", "col", None),
        P("lag", "col"),
    )
    return jax.shard_map(
        shards,
        mesh=mesh,
        in_specs=placed,
        out_specs=P("lag", "col", None, None, None),
        check_vma=False,
    )
```

```python
import jax
import jax.numpy as jnp
from jax import lax
from jax.experimental import pallas as pl
from jax.experimental.pallas import tpu as pltpu
from jax.sharding import PartitionSpec as P

ITERS = 12
REACH = 4
RELAXATION = 0.9
EPSILON = 1e-06
MEMBERS = 128
HALF = MEMBERS // 2
PACKED = 72
PAIR = PACKED + HALF

bf16 = jnp.bfloat16
f32 = jnp.float32


def iota2(shape, dim):
    return lax.broadcasted_iota(jnp.int32, shape, dim)


def halves(value):
    high = value.astype(bf16)
    return high, (value - high.astype(f32)).astype(bf16)


def dot(left, right):
    return jnp.dot(left, right, preferred_element_type=f32)


def crossed_halves(high, low):
    return jnp.concatenate(
        [jnp.concatenate([high, low], axis=1), jnp.concatenate([low, high], axis=1)], axis=0
    )


def cross(right):
    return crossed_halves(*halves(right))


def product(left, crossed):
    both = dot(jnp.concatenate(halves(left), axis=1), crossed)
    return both[:, :MEMBERS] + both[:, MEMBERS:]


def pack(gram, vector):
    row, lane = iota2((HALF, MEMBERS), 0), iota2((HALF, MEMBERS), 1)
    lower = pltpu.roll(gram[HALF:], HALF, 1)
    matrix = jnp.where(lane >= row, gram[:HALF], lower)
    diagonal = jnp.sum(jnp.where(lane == row, lower, 0.0), axis=0, keepdims=True)
    tail = iota2((8, MEMBERS), 0)
    rest = jnp.where(tail == 0, diagonal, jnp.where(tail == 1, vector, 0.0))
    return jnp.concatenate([matrix, rest], axis=0)


def unpack(matrix, rest):
    row, lane = iota2((HALF, MEMBERS), 0), iota2((HALF, MEMBERS), 1)
    diagonal, vector = rest[0:1], rest[1:2]
    flipped = jnp.transpose(jnp.concatenate([matrix, jnp.zeros_like(matrix)], axis=0))
    upper = jnp.where(lane >= row, matrix, flipped[:HALF])
    corner = jnp.where(lane == row, diagonal, jnp.where(lane < row, matrix, flipped[:HALF]))
    lower = jnp.where(lane < HALF, flipped[HALF:], pltpu.roll(corner, HALF, 1))
    return jnp.concatenate([upper, lower], axis=0), vector


def statistics_kernel(
    count_hbm, weight_hbm, value_hbm, ensemble_hbm, out_ref,
    count_ref, weight_ref, value_ref, ensemble_ref, system_ref, sem,
):
    patches = ensemble_ref.shape[0]
    arrays = [(count_hbm, count_ref), (weight_hbm, weight_ref), (value_hbm, value_ref)]
    parts = [(ensemble_hbm, ensemble_ref)]
    copies = [
        pltpu.make_async_copy(source, target, sem.at[i])
        for i, (source, target) in enumerate(parts + arrays)
    ]
    for copy in copies:
        copy.start()
    for copy in copies[1:]:
        copy.wait()
    lane = iota2((1, MEMBERS), 1)
    copies[0].wait()
    for p in range(patches):
        weight = weight_ref[p : p + 1, :].astype(f32)
        weight = jnp.sqrt(jnp.where(lane < count_ref[:, p : p + 1], weight, 0.0))
        flipped = jnp.transpose(ensemble_ref[p].astype(f32))
        center = jnp.sum(flipped, axis=0, keepdims=True) * (1.0 / MEMBERS)
        spread = flipped - center
        innovation = value_ref[p : p + 1, :].astype(f32) - center
        innovation = jnp.broadcast_to(innovation, (16, MEMBERS))
        high, low = halves(jnp.concatenate([spread, innovation], axis=0) * weight)
        both = lax.dot_general(
            jnp.concatenate([high, low], axis=1),
            crossed_halves(high[:MEMBERS], low[:MEMBERS]),
            (((1,), (1,)), ((), ())),
            preferred_element_type=f32,
        )
        sums = both[:, :MEMBERS] + both[:, MEMBERS:]
        system_ref[p] = pack(sums[:MEMBERS], sums[MEMBERS : MEMBERS + 1])

    def tapered(target):
        total = None
        for p in range(patches):
            distance = abs(target - p)
            if distance <= REACH:
                term = (1.0 - distance / (REACH + 1.0)) * system_ref[p]
                total = term if total is None else total + term
        return total

    for lag in range(patches):
        own = tapered(lag)
        beside = tapered(lag + patches if lag < REACH else lag - patches)
        out_ref[lag, :HALF] = own[:HALF]
        out_ref[lag, HALF:MEMBERS] = beside[:HALF]
        out_ref[lag, MEMBERS:] = own[HALF:] + pltpu.roll(beside[HALF:], 2, 0)


VMEM = pl.BlockSpec(memory_space=pltpu.VMEM)
HBM = pl.BlockSpec(memory_space=pltpu.HBM)
PARAMS = pltpu.CompilerParams(vmem_limit_bytes=16 * 1024 * 1024)


def statistics(obs_count, obs_weight, obs_value, obs_ensemble):
    patches, observations, members = obs_ensemble.shape
    operands = (obs_count, obs_weight, obs_value, obs_ensemble)
    operands = [pltpu.with_memory_space_constraint(x, pltpu.HBM) for x in operands]
    return pl.pallas_call(
        statistics_kernel,
        out_shape=jax.ShapeDtypeStruct((patches, PAIR, members), f32),
        in_specs=[HBM] * 4,
        out_specs=VMEM,
        scratch_shapes=[
            pltpu.VMEM(obs_count.shape, jnp.int32),
            pltpu.VMEM(obs_weight.shape, bf16),
            pltpu.VMEM(obs_value.shape, bf16),
            pltpu.VMEM(obs_ensemble.shape, bf16),
            pltpu.VMEM((patches, PACKED, members), f32),
            pltpu.SemaphoreType.DMA((4,)),
        ],
        compiler_params=PARAMS,
    )(*operands)


def solver_kernel(received_ref, beside_ref, out_ref):
    matrix = beside_ref[:HALF]
    rest = pltpu.roll(beside_ref[HALF:], 6, 0)
    for s in range(received_ref.shape[0]):
        matrix = matrix + received_ref[s, :HALF]
        rest = rest + received_ref[s, MEMBERS:]
    gram, vector = unpack(matrix, rest)
    shape = (MEMBERS, MEMBERS)
    identity = jnp.where(iota2(shape, 0) == iota2(shape, 1), 1.0, 0.0)
    matrix = gram + (MEMBERS - 1.0) * identity
    bound = jnp.sum(jnp.sum(jnp.abs(matrix), axis=0, keepdims=True), axis=1, keepdims=True)
    state = matrix / bound
    inverse_root = None
    for sweep in range(ITERS):
        middle = 1.5 * identity - 0.5 * state
        crossed = cross(middle)
        if sweep < ITERS - 1:
            state = product(product(state, crossed), crossed)
        inverse_root = middle if sweep == 0 else product(inverse_root, crossed)
    inner = jnp.sum(inverse_root * vector, axis=1, keepdims=True)
    mean_weight = jnp.sum(inverse_root * inner, axis=0, keepdims=True) / bound
    mean_weight = jnp.sum(jnp.where(identity > 0.0, mean_weight, 0.0), axis=1, keepdims=True)
    mixing = inverse_root * jnp.sqrt((MEMBERS - 1.0) / bound) + mean_weight
    out_ref[...] = jnp.broadcast_to(mixing.astype(bf16)[None], out_ref.shape)


def solver(received, beside):
    return pl.pallas_call(
        solver_kernel,
        out_shape=jax.ShapeDtypeStruct((received.shape[0], MEMBERS, MEMBERS), bf16),
        in_specs=[VMEM, VMEM],
        out_specs=VMEM,
        compiler_params=PARAMS,
    )(received, beside)


def level_sums(squares, levels):
    return jnp.sum(squares.reshape(levels, -1, 8, MEMBERS), axis=1)


def prior_kernel(states_ref, spread_ref, center_ref, square_ref):
    patches, levels, columns, _ = states_ref.shape
    average = jnp.full((MEMBERS, MEMBERS), 1.0 / MEMBERS, bf16)
    total = None
    for p in range(patches):
        states = states_ref[p].reshape(levels * columns, MEMBERS)
        center = dot(states, average)
        spread = (states.astype(f32) - center).astype(bf16)
        spread_ref[p] = spread
        center_ref[p] = center
        square = level_sums(jnp.square(spread.astype(f32)), levels)
        total = square if total is None else total + square
    square_ref[...] = total


def prior(states):
    patches, levels, columns, members = states.shape
    rows = levels * columns
    return pl.pallas_call(
        prior_kernel,
        out_shape=(
            jax.ShapeDtypeStruct((patches, rows, members), bf16),
            jax.ShapeDtypeStruct((patches, rows, members), f32),
            jax.ShapeDtypeStruct((levels, 8, members), f32),
        ),
        in_specs=[VMEM],
        out_specs=(VMEM, VMEM, VMEM),
        compiler_params=PARAMS,
        cost_estimate=pl.CostEstimate(
            flops=2 * patches * rows * members * members, bytes_accessed=1 << 22, transcendentals=0
        ),
    )(states)


def apply_kernel(mixing_ref, prior_spread_ref, prior_center_ref, prior_square_ref, spread_ref, center_ref, sums_ref):
    patches = mixing_ref.shape[0]
    levels = prior_square_ref.shape[0]
    centers = [
        jnp.broadcast_to(
            jnp.sum(mixing_ref[p].astype(f32), axis=1, keepdims=True) * (1.0 / MEMBERS),
            (MEMBERS, MEMBERS),
        )
        for p in range(patches)
    ]
    rights = []
    for p in range(patches):
        spread_high, spread_low = halves(mixing_ref[p].astype(f32) - centers[p])
        center_high, center_low = halves(centers[p])
        rights.append(
            jnp.concatenate(
                [
                    jnp.concatenate([spread_high, center_high], axis=1),
                    jnp.concatenate([spread_low, center_low], axis=1),
                ],
                axis=0,
            )
        )
    total = None
    for p in range(patches):
        prior_spread = prior_spread_ref[p]
        both = dot(jnp.concatenate([prior_spread, prior_spread], axis=1), rights[p])
        post_spread = both[:, :MEMBERS]
        spread_ref[p] = post_spread
        center_ref[p] = prior_center_ref[p] + both[:, MEMBERS:]
        square = level_sums(jnp.square(post_spread), levels)
        total = square if total is None else total + square
    sums = jnp.concatenate(
        [jnp.sum(prior_square_ref[...], axis=1), jnp.sum(total, axis=1),
         jnp.zeros((MEMBERS - 2 * levels, MEMBERS), f32)], axis=0
    )
    sums = jnp.sum(jnp.transpose(sums), axis=0, keepdims=True)
    sums_ref[...] = jnp.broadcast_to(sums, sums_ref.shape)


def apply_weights(mixing, prior_spread, prior_center, prior_square, receivers):
    patches, rows, members = prior_spread.shape
    return pl.pallas_call(
        apply_kernel,
        out_shape=(
            jax.ShapeDtypeStruct((patches, rows, members), f32),
            jax.ShapeDtypeStruct((patches, rows, members), f32),
            jax.ShapeDtypeStruct((receivers, members), f32),
        ),
        in_specs=[VMEM] * 4,
        out_specs=(VMEM, VMEM, VMEM),
        compiler_params=PARAMS,
    )(mixing, prior_spread, prior_center, prior_square)


def finish_kernel(divisor, sums_ref, spread_ref, center_ref, out_hbm, out_ref, out_sem):
    patches, levels, columns, _ = out_ref.shape
    sums = jnp.sum(sums_ref[...], axis=0, keepdims=True)
    deviation = jnp.sqrt(sums / divisor + EPSILON)
    lane = iota2(deviation.shape, 1)
    factors = []
    for level in range(levels):
        prior_sd = jnp.sum(jnp.where(lane == level, deviation, 0.0), axis=1, keepdims=True)
        post_sd = jnp.sum(jnp.where(lane == levels + level, deviation, 0.0), axis=1, keepdims=True)
        factors.append(1.0 + RELAXATION * (prior_sd - post_sd) / post_sd)
    copies = []
    for p in range(patches):
        for level in range(levels):
            rows = pl.ds(level * columns, columns)
            result = center_ref[p, rows] + factors[level] * spread_ref[p, rows]
            out_ref[p, level] = result.astype(bf16)
        copies.append(pltpu.make_async_copy(out_ref.at[p], out_hbm.at[p], out_sem.at[p]))
        copies[-1].start()
    for copy in copies:
        copy.wait()


def finish(sums, spread, center, shape, divisor):
    def kernel(*refs):
        finish_kernel(divisor, *refs)

    return pl.pallas_call(
        kernel,
        out_shape=jax.ShapeDtypeStruct(shape, bf16),
        in_specs=[VMEM] * 3,
        out_specs=HBM,
        scratch_shapes=[pltpu.VMEM(shape, bf16), pltpu.SemaphoreType.DMA((shape[0],))],
        compiler_params=PARAMS,
    )(sums, spread, center)


def shards(background, obs_ensemble, obs_value, obs_weight, obs_count):
    lags, tiles = lax.axis_size("lag"), lax.axis_size("col")
    patches, columns = background.shape[1], background.shape[3]
    sent = statistics(obs_count, obs_weight[0], obs_value[0], obs_ensemble[0])
    received = lax.all_to_all(sent, "lag", 0, 0)
    beside = jnp.sum(received[:, HALF:], axis=0)
    moves = [
        (i * tiles + c, i * tiles + (c + (1 if i < REACH else -1)) % tiles)
        for i in range(lags)
        for c in range(tiles)
    ]
    states, beside = lax.optimization_barrier((background[0], beside))
    beside = lax.ppermute(beside, ("lag", "col"), moves)
    prior_spread, prior_center, prior_square = prior(states)
    beside, prior_square = lax.optimization_barrier((beside, prior_square))
    mixing = lax.all_to_all(solver(received, beside), "lag", 0, 0)
    spread, center, sums = apply_weights(mixing, prior_spread, prior_center, prior_square, tiles)
    sums = lax.all_to_all(sums, "col", 0, 0, tiled=True)
    divisor = (MEMBERS - 1.0) * patches * tiles * columns
    return finish(sums, spread, center, background.shape[1:], divisor)[None]


def solution(mesh):
    placed = (
        P("lag", "col", None, None, None),
        P("lag", "col", None, None),
        P("lag", "col", None),
        P("lag", "col", None),
        P("lag", "col"),
    )
    return jax.shard_map(
        shards,
        mesh=mesh,
        in_specs=placed,
        out_specs=P("lag", "col", None, None, None),
        check_vma=False,
    )
```
